128 devices in a mesh: dp: 32 (over x_lo, z, y), seq: 4 (over x_hi, core).
Axes of the slice: x: 4 (x_hi: 2, x_lo: 2; x = x_hi * 2 + x_lo), y: 4, z: 4, core: 2. Of those that a mesh axis runs over, the one named last changes fastest.
Arguments:
- latents: bfloat16 [65536, 3072], P(('dp', 'seq')), may hold values from -6 to 6
- target: int32 [65536], P(('dp', 'seq')), may hold values from 0 to 65535, as said below
- segment_ids: int32 [32, 2048], P('dp', 'seq'), may hold values from 0 to 7, never falling along the last dimension, each value on 1 to 512 neighbouring positions
- clip_bucket: int32 [32, 8], P('dp'), may hold values from 0 to 15
- mod_table: bfloat16 [16, 6144], replicated, may hold values from -3 to 3
- w_query: bfloat16 [3072, 1536], P('dp', 'seq')
- w_key: bfloat16 [3072, 1536], P('dp', 'seq')
- w_value: bfloat16 [3072, 1536], P('dp', 'seq'), may hold values from -0.109375 to 0.109375
Outputs:
- attended: bfloat16 [65536, 1536], P(('dp', 'seq'))
The draws below stay inside these ranges and needn't reach their ends.
Inputs may be any that keep to these rules, and one draw needn't show every extreme that they name: `target`: a permutation of 0 to 65535; a token stays at the same index of seq; a device sends at most 24 tokens to one index of dp, exactly 24 to some index in every draw, and sends to at most (535) // 24 + 1 indices.
All inputs are finite; a program needn't handle non-finite values.
Results may differ from the reference program's by a relative error of at most 0.0051.
Values may be sent and summed in bfloat16 or wider, within the bound.
A program may use at most 128 MiB of HBM per device.

```python
import math
import jax
import jax.numpy as jnp
import numpy as np
from jax import lax

D = 3072
HEADS = 12
HEAD_DIM = 128
CLIPS = 8
BUCKETS = 16
TOK_DEV = 512
SEQ_LEN = 2048
TOKENS = 65536
CAP = 24
N_DP = 32
N_SEQ = 4


def shared_rows(key):
    return jax.random.normal(key, (D, HEADS * HEAD_DIM), jnp.float32) * D ** (-0.5)


def draw_w_query(key, part):
    shared = shared_rows(key)
    return shared.astype(jnp.bfloat16)


def draw_w_key(key, part):
    key = jax.random.fold_in(key, 7)
    independent = jax.random.normal(key, (D, HEADS * HEAD_DIM), jnp.float32) * D ** (-0.5)
    return independent.astype(jnp.bfloat16)


def plan_column(key, column):
    subkeys = jax.random.split(key, 3)
    route_count = (TOK_DEV + CAP - 1) // CAP + 1
    shifts = jax.random.permutation(subkeys[0], N_DP)[:route_count]
    remaining = TOK_DEV - CAP
    base_count = remaining // (route_count - 1)
    extra_count = remaining % (route_count - 1)
    later = base_count + (jnp.arange(route_count - 1) < extra_count).astype(jnp.int32)
    counts = jnp.concatenate([jnp.full((1,), CAP, jnp.int32), later.astype(jnp.int32)])
    group_ends = jnp.cumsum(counts)
    ordered = jnp.arange(TOK_DEV)
    group_of = jnp.sum((ordered[:, None] >= group_ends[None, :]).astype(jnp.int32), axis=1)
    senders = jnp.arange(N_DP)
    receiver = (senders[:, None] + shifts[group_of][None, :]) % N_DP
    source_rows = jax.vmap(lambda sub: jax.random.permutation(sub, TOK_DEV))(jax.random.split(subkeys[1], N_DP))
    final_rows = jax.vmap(lambda sub: jax.random.permutation(sub, TOK_DEV))(jax.random.split(subkeys[2], N_DP))
    landing = final_rows[receiver, ordered[None, :]]
    landing_row = (receiver * N_SEQ + column) * TOK_DEV + landing
    plan_table = jnp.zeros((N_DP, TOK_DEV), jnp.int32)
    plan_table = plan_table.at[senders[:, None], source_rows].set(landing_row.astype(jnp.int32))
    return plan_table


def draw_target(key, part):
    key = jax.random.fold_in(key, 3)
    columns = [plan_column(jax.random.fold_in(key, column), column) for column in range(N_SEQ)]
    stacked = jnp.stack(columns, axis=1)
    return stacked.reshape(N_DP * N_SEQ * TOK_DEV)


def with_ends(values, own_key, least, largest):
    longest = values.shape.index(max(values.shape))
    spots = []
    for shift in (0, 1):
        where = [jax.random.randint(jax.random.fold_in(own_key, axis), (), 0, length) for axis, length in enumerate(values.shape)]
        where[longest] = (where[longest] + shift) % values.shape[longest]
        spots.append(tuple(where))
    return values.at[spots[0]].set(least).at[spots[1]].set(largest)


def block_levels(key, extent, cuts, low, largest):
    def one(dim, blocks):
        steps = jax.random.uniform(jax.random.fold_in(jax.random.fold_in(key, 6), dim), (blocks,), jnp.float32, low / len(cuts), largest / len(cuts))
        return jnp.repeat(jnp.exp(steps), extent[dim] // blocks).reshape((-1,) + (1,) * (len(extent) - dim - 1))

    loudness = one(*cuts[0])
    for cut in cuts[1:]:
        loudness = loudness * one(*cut)
    return loudness


def split_up(amount, total, bound, lean):
    portions = [(1 << 20) // math.isqrt(standing ** lean) + 1 for standing in range(2, amount + 1)]
    spare, given = total - bound - (amount - 1), [1] * (amount - 1)
    while spare > 0:
        candidates = [i for i in range(amount - 1) if given[i] < bound]
        pool, left = sum([portions[i] for i in candidates]), spare
        for i in candidates:
            more = min(bound - given[i], max(1, left * portions[i] // pool), spare)
            given[i] = given[i] + more
            spare = spare - more
    return np.array([bound] + given)


def uneven_parts(key, count, total, most, slope):
    if count == 2:
        one = jax.random.randint(key, (), max(1, total - most), min(most, total - 1) + 1)
        return jnp.stack([one, total - one])
    tallies = jnp.asarray(split_up(count, total, most, slope), jnp.int32)
    pairs = (count - 1) // 2
    giver, taker = tallies[1:1 + 2 * pairs:2], tallies[2:2 + 2 * pairs:2]
    room = jnp.minimum(giver - 1, most - taker)
    shifted = jax.random.randint(jax.random.fold_in(key, 1), (pairs,), 0, 1 << 20) % (room + 1)
    tallies = tallies.at[1:1 + 2 * pairs:2].set(giver - shifted).at[2:2 + 2 * pairs:2].set(taker + shifted)
    return tallies[jax.random.permutation(jax.random.fold_in(key, 2), count)]


def normal_values(stream_key, shape, spread, limit, cuts=(), held_as=jnp.bfloat16):
    entries = spread * jax.random.normal(stream_key, shape, jnp.float32)
    if cuts:
        entries = entries * block_levels(stream_key, shape, cuts, -0.22, 0.18)
    return jnp.clip(entries, -limit, limit).astype(held_as)


def setup_inputs(seed: int = 0) -> dict:
    seeds = jax.random.split(jax.random.key(seed), 9)
    return {
        "latents": normal_values(seeds[0], (TOKENS, D), 1.0, 6.0, ((0, 128),)),
        "target": draw_target(jax.random.fold_in(seeds[8], 71), 0),
        "segment_ids": jax.vmap(lambda own: jnp.searchsorted(jnp.cumsum(uneven_parts(own, CLIPS, SEQ_LEN, SEQ_LEN // 4, 2)), jnp.arange(SEQ_LEN), side="right"))(jax.random.split(seeds[2], N_DP)).reshape((N_DP, SEQ_LEN)).astype(jnp.int32),
        "clip_bucket": with_ends(jax.random.randint(seeds[3], (N_DP, CLIPS), 0, BUCKETS), jax.random.fold_in(seeds[3], 1), 0, BUCKETS - 1).astype(jnp.int32),
        "mod_table": normal_values(seeds[4], (BUCKETS, 2 * D), 0.5, 3.0),
        "w_query": draw_w_query(jax.random.fold_in(seeds[8], 71), 0),
        "w_key": draw_w_key(jax.random.fold_in(seeds[8], 71), 0),
        "w_value": normal_values(seeds[7], (D, HEADS * HEAD_DIM), D ** -0.5, 0.109375, ((0, 32), (1, 4))),
    }


def modulated_norm(latent_rows, token_bucket, mod_table):
    width = latent_rows.shape[1]
    modulation = mod_table[token_bucket].astype(jnp.float32)
    shift_part = modulation[:, :width]
    scale_part = modulation[:, width:]
    widened = latent_rows.astype(jnp.float32)
    row_mean = lax.optimization_barrier(jnp.mean(widened, axis=1, keepdims=True))
    centered = widened - row_mean
    row_var = lax.optimization_barrier(jnp.mean(centered * centered, axis=1, keepdims=True))
    normalized = centered * lax.rsqrt(row_var + 1e-06)
    return (normalized * (1.0 + scale_part) + shift_part).astype(jnp.bfloat16)

def reference(latents, target, segment_ids, clip_bucket, mod_table, w_query, w_key, w_value):
    placed = jnp.zeros_like(latents).at[target].set(latents)
    grouped = placed.reshape(N_DP, SEQ_LEN, D)
    factor = HEAD_DIM ** (-0.5)

    def group_attention(inputs):
        latent_rows, segment_row, bucket_row = inputs
        token_bucket = bucket_row[segment_row]
        hidden = modulated_norm(latent_rows, token_bucket, mod_table)
        query = jnp.dot(hidden, w_query, preferred_element_type=jnp.float32).astype(jnp.bfloat16)
        keys = jnp.dot(hidden, w_key, preferred_element_type=jnp.float32).astype(jnp.bfloat16)
        values = jnp.dot(hidden, w_value, preferred_element_type=jnp.float32).astype(jnp.bfloat16)
        query = query.reshape(SEQ_LEN, HEADS, HEAD_DIM).astype(jnp.float32)
        keys = keys.reshape(SEQ_LEN, HEADS, HEAD_DIM).astype(jnp.float32)
        values = values.reshape(SEQ_LEN, HEADS, HEAD_DIM).astype(jnp.float32)
        scores = jnp.einsum('qhd,khd->hqk', query, keys) * factor
        same_clip = segment_row[:, None] == segment_row[None, :]
        scores = jnp.where(same_clip[None, :, :], scores, -1e+30)
        row_max = lax.optimization_barrier(jnp.max(scores, axis=2, keepdims=True))
        exponent = jnp.exp(scores - row_max)
        row_total = lax.optimization_barrier(jnp.sum(exponent, axis=2, keepdims=True))
        probs = (exponent / row_total).astype(jnp.bfloat16)
        result = jnp.einsum('hqk,khd->qhd', probs.astype(jnp.float32), values)
        return result.reshape(SEQ_LEN, HEADS * HEAD_DIM).astype(jnp.bfloat16)
    attended = lax.map(group_attention, (grouped, segment_ids, clip_bucket))
    return attended.reshape(TOKENS, HEADS * HEAD_DIM)
```

```python
import functools

import jax
import jax.numpy as jnp
from jax import lax
from jax.experimental import pallas as pl
from jax.experimental.pallas import tpu as pltpu
from jax.sharding import PartitionSpec as P

MESH = pl.DeviceIdType.MESH
F32, BF16, I32 = jnp.float32, jnp.bfloat16, jnp.int32
ROWS, WIDTH, HALF, HEAD_DIM = 512, 3072, 1536, 128
BLOCK = WIDTH + HALF + 128
KEY, VALUE, QUERY = 0, 1, 2
PARTS = (
    (KEY, 0, (0, 1, 2)),
    (KEY, 1, (0, 2, 1)),
    (VALUE, 0, (0, 1, 2)),
    (VALUE, 1, (2, 0, 1)),
    (QUERY, 0, (0, 1, 2)),
    (QUERY, 1, (2, 1, 0)),
)


def dot(a, b):
    return jnp.dot(a, b, preferred_element_type=F32)


def dot_nt(a, b):
    return lax.dot_general(a, b, (((1,), (1,)), ((), ())), preferred_element_type=F32)


def iota(shape, dim):
    return lax.broadcasted_iota(I32, shape, dim)


def one_hot(row_ids, lane_ids):
    return jnp.where(row_ids == lane_ids, 1.0, 0.0).astype(BF16)


def project_kernel(
    target, segment, bucket, mod_table, latents, w_query, w_key, w_value,
    q_out, k_out, v_out, seg_out,
    outgoing, incoming, weights, hidden, tags, hits, keys, seg_all,
    a_send, a_recv, w_send, w_recv, s_send, s_recv, x_send, x_recv, h_send, h_recv, f_send, f_recv, local,
):
    me_dp, me_seq = lax.axis_index("dp"), lax.axis_index("seq")
    x_lo, z, y = me_dp // 16, (me_dp // 4) % 4, me_dp % 4
    x_hi, core = me_seq // 2, me_seq % 2
    me = (x_hi * 2 + x_lo, z, y)
    sibling = (me_dp, x_hi * 2 + (1 - core))

    def at_chip(c):
        return ((c[0] % 2) * 16 + c[1] * 4 + c[2], (c[0] // 2) * 2 + core)

    def at_block(b, sign):
        r = (13 * b) % 32
        dz, dy = (r // 4) % 4, r % 4
        return (((x_lo + r // 16) % 2) * 16 + ((z + 4 + sign * dz) % 4) * 4 + (y + 4 + sign * dy) % 4, me_seq)

    def seq_peer(r):
        if r == 1:
            return sibling
        return (me_dp, (1 - x_hi) * 2 + (core if r == 2 else 1 - core))

    barrier = pltpu.get_barrier_semaphore()

    def greet(k, carry):
        pl.semaphore_signal(barrier, inc=1, device_id=((me_dp + k) % 32, me_seq), device_id_type=MESH)
        return carry

    lax.fori_loop(1, 32, greet, 0)
    for peer in (seq_peer(1), seq_peer(2), seq_peer(3), ((1 - x_lo) * 16 + z * 4 + y, (1 - x_hi) * 2 + core)):
        pl.semaphore_signal(barrier, inc=1, device_id=peer, device_id_type=MESH)

    own = []
    for m, shard in ((KEY, w_key), (VALUE, w_value), (QUERY, w_query)):
        copy = pltpu.make_async_copy(shard, weights.at[m, me[0], z, y], local.at[m])
        copy.start()
        own.append(copy)
    seg_all[me_seq] = jnp.broadcast_to(segment[...], (8, ROWS))
    for copy in own:
        copy.wait()
    pl.semaphore_wait(barrier, 35)

    def w_copy(p, phase, pos, off):
        m, half, order = PARTS[p]
        axis, done = order[phase], order[:phase]
        index = [m]
        for ax in range(3):
            index.append(pos % 4 if ax == axis else slice(None) if ax in done else me[ax])
        index.append(pl.ds(48 * half, 48))
        there = list(me)
        there[axis] = (there[axis] + off) % 4
        piece = weights.at[tuple(index)]
        return pltpu.make_async_remote_copy(
            src_ref=piece, dst_ref=piece, send_sem=w_send.at[p, phase, off - 1], recv_sem=w_recv.at[p, phase, off - 1],
            device_id=at_chip(there), device_id_type=MESH,
        )

    def w_start(p, phase):
        axis = PARTS[p][2][phase]
        for off in (1, 3, 2):
            w_copy(p, phase, me[axis], off).start()

    def w_arrived(p, phase):
        axis = PARTS[p][2][phase]
        for off in (1, 3, 2):
            w_copy(p, phase, me[axis] + 4 - off, off).wait_recv()

    for p in range(6):
        w_start(p, 0)

    def s_copy(r, slot):
        return pltpu.make_async_remote_copy(
            src_ref=seg_all.at[slot], dst_ref=seg_all.at[slot], send_sem=s_send.at[r - 1], recv_sem=s_recv.at[r - 1],
            device_id=seq_peer(r), device_id_type=MESH,
        )

    for r in (1, 2, 3):
        s_copy(r, me_seq).start()

    row = target[...] & (ROWS - 1)
    dest = target[...] >> 11
    rel = (((dest >> 4) + x_lo) & 1) * 16 + ((((dest >> 2) & 3) + 4 - z) & 3) * 4 + (((dest & 3) + 4 - y) & 3)
    block = (5 * rel) & 31
    block_hit = jnp.where(iota((32, ROWS), 0) == block, 1.0, 0.0)
    before = one_hot(jnp.minimum(iota((ROWS, ROWS), 0) + 1, iota((ROWS, ROWS), 1)), iota((ROWS, ROWS), 0) + 1)
    earlier = dot(block_hit.astype(BF16), before)
    rank = jnp.sum(block_hit * earlier, axis=0, keepdims=True).astype(I32)
    late = rank >= 16
    keys[0:1] = jnp.where(late, -1, block * 16 + rank)
    keys[1:2] = jnp.where(late, block * 16 + rank - 16, -1)
    keys[2:3] = jnp.where(late, block * 16 + rank - 8, -1)
    token_bucket = jnp.zeros((1, ROWS), I32)
    for clip in range(8):
        token_bucket += jnp.where(segment[...] == clip, bucket[:, clip : clip + 1], 0)
    stacked = jnp.concatenate([row.astype(F32), token_bucket.astype(F32), jnp.zeros((6, ROWS), F32)], axis=0)
    columns = jnp.transpose(stacked)
    row_col, bucket_col = columns[:, 0:1], columns[:, 1:2]
    lane = iota((ROWS, 128), 1)
    hits[...] = jnp.where(bucket_col == lane.astype(F32), 1.0, 0.0).astype(BF16)
    high = jnp.where(row_col >= 256.0, 1.0, 0.0)
    low = row_col - 256.0 * high
    kind = lane % 3
    tag = jnp.where(kind == 0, low, jnp.where(kind == 1, high, 1.0))
    tags[0] = jnp.where(lane < 3, tag, 0.0).astype(BF16)
    tags[1] = jnp.where((lane >= 3) & (lane < 6), tag, 0.0).astype(BF16)

    def pack(c, carry):
        base = pl.multiple_of(c * 128, 128)
        rows = pl.ds(base, 128)
        ids = iota((128, ROWS), 0) + base
        first = one_hot(ids, keys[0:1])
        left = one_hot(ids, keys[1:2])
        right = one_hot(ids, keys[2:3])
        outgoing[rows, 0:WIDTH] = dot(first, latents[...]).astype(BF16)
        outgoing[rows, WIDTH : WIDTH + HALF] = (dot(left, latents[:, 0:HALF]) + dot(right, latents[:, HALF:WIDTH])).astype(BF16)
        outgoing[rows, WIDTH + HALF : BLOCK] = (dot(first, tags[0]) + dot(left + right, tags[1])).astype(BF16)
        return carry

    lax.fori_loop(0, 4, pack, 0)

    for p in range(6):
        w_arrived(p, 0)
        w_start(p, 1)

    def a_copy(b, sign):
        rows = pl.ds(pl.multiple_of(b * 16, 16), 16)
        return pltpu.make_async_remote_copy(
            src_ref=outgoing.at[rows], dst_ref=incoming.at[rows], send_sem=a_send.at[b], recv_sem=a_recv.at[b],
            device_id=at_block(b, sign), device_id_type=MESH,
        )

    def a_start(b, carry):
        a_copy(b, 1).start()
        return carry

    def a_wait(b, carry):
        a_copy(b, -1).wait()
        return carry

    lax.fori_loop(1, 32, a_start, 0)
    incoming[0:16] = outgoing[0:16]
    for p in range(6):
        w_arrived(p, 1)
        w_start(p, 2)
    lax.fori_loop(1, 32, a_wait, 0)

    own_slot, sib_slot, halo_slot = x_hi + core, x_hi + 1 - core, 2 - 2 * x_hi
    pick_lane = iota((8, 128), 1)
    pick_row = iota((8, 128), 0)
    pick_kind = pick_lane - 3 * pick_row
    pick = jnp.where(
        pick_row < 2,
        jnp.where(pick_kind == 0, 1.0, jnp.where(pick_kind == 1, 256.0, jnp.where(pick_kind == 2, 512.0, 0.0))),
        0.0,
    ).astype(BF16)
    rows_in = dot_nt(pick, incoming[:, WIDTH + HALF : BLOCK]).astype(I32) - 512
    odd = (iota((1, ROWS), 1) & 15) >= 8
    keys[0:1] = rows_in[0:1]
    keys[1:2] = jnp.where(odd, -1, rows_in[1:2])
    keys[2:3] = jnp.where(odd, rows_in[1:2], -1)

    def chunk(slot, c):
        return hidden.at[slot, pl.ds(pl.multiple_of(c * 128, 128), 128)]

    def x_copy(slot, c):
        return pltpu.make_async_remote_copy(
            src_ref=chunk(slot, c), dst_ref=chunk(slot, c), send_sem=x_send.at[c], recv_sem=x_recv.at[c],
            device_id=sibling, device_id_type=MESH,
        )

    def h_copy(c):
        return pltpu.make_async_remote_copy(
            src_ref=chunk(own_slot, c), dst_ref=chunk(2 * x_hi, c), send_sem=h_send.at[c], recv_sem=h_recv.at[c % 2],
            device_id=(me_dp, (1 - x_hi) * 2 + c // 2), device_id_type=MESH,
        )

    def f_copy(i, owner):
        c = 2 * owner + i
        return pltpu.make_async_remote_copy(
            src_ref=chunk(halo_slot, c), dst_ref=chunk(halo_slot, c), send_sem=f_send.at[i], recv_sem=f_recv.at[i],
            device_id=sibling, device_id_type=MESH,
        )

    on_edge = x_hi + core == 1

    def place(c, carry):
        base = pl.multiple_of(c * 128, 128)
        rows = pl.ds(base, 128)
        ids = iota((128, ROWS), 0) + base
        whole = dot(one_hot(ids, keys[0:1]), incoming[:, 0:WIDTH])
        left = dot(one_hot(ids, keys[1:2]), incoming[:, WIDTH : WIDTH + HALF])
        right = dot(one_hot(ids, keys[2:3]), incoming[:, WIDTH : WIDTH + HALF])
        placed = whole + jnp.concatenate([left, right], axis=1)
        centered = placed - jnp.mean(placed, axis=1, keepdims=True)
        var = jnp.mean(centered * centered, axis=1, keepdims=True)
        normalized = centered * lax.rsqrt(var + 1e-6)
        modulation = dot(hits[rows, 0:16], mod_table[...])
        hidden[own_slot, rows] = (normalized * (1.0 + modulation[:, WIDTH:]) + modulation[:, :WIDTH]).astype(BF16)
        x_copy(own_slot, c).start()

        @pl.when(on_edge)
        def _():
            h_copy(c).start()

        return carry

    lax.fori_loop(0, 4, place, 0)

    def project(m, out, slot, out_base):
        def step(s, carry):
            r, h = s // 2, s % 2
            w = weights[m, pl.ds(2 * h, 2)].reshape(WIDTH, 384)
            rows = pl.ds(pl.multiple_of(r * 256, 256), 256)
            result = dot(hidden[slot, rows], w).astype(BF16)
            out[pl.ds(pl.multiple_of(out_base + r * 256, 256), 256), pl.ds(pl.multiple_of(h * 384, 128), 384)] = result
            return carry

        lax.fori_loop(0, 4, step, 0)

    for p in (0, 1):
        w_arrived(p, 2)
    project(KEY, k_out, own_slot, own_slot * 512)
    for c in range(4):
        x_copy(sib_slot, c).wait_recv()
    project(KEY, k_out, sib_slot, sib_slot * 512)
    for i in range(2):
        h_copy(2 * core + i).wait_recv()
        f_copy(i, core).start()
    for p in (2, 3):
        w_arrived(p, 2)
    project(VALUE, v_out, own_slot, own_slot * 512)
    project(VALUE, v_out, sib_slot, sib_slot * 512)
    for i in range(2):
        f_copy(i, 1 - core).wait_recv()
    project(KEY, k_out, halo_slot, halo_slot * 512)
    project(VALUE, v_out, halo_slot, halo_slot * 512)
    for p in (4, 5):
        w_arrived(p, 2)
    project(QUERY, q_out, own_slot, core * 512)
    project(QUERY, q_out, sib_slot, (1 - core) * 512)

    for r in (1, 2, 3):
        s_copy(r, (seq_peer(r)[1])).wait_recv()
    for i in range(3):
        seg_out[:, 512 * i : 512 * i + 512] = seg_all[x_hi + i]

    for r in (1, 2, 3):
        s_copy(r, me_seq).wait_send()
    for p in range(6):
        for phase in range(3):
            for off in (1, 3, 2):
                w_copy(p, phase, me[PARTS[p][2][phase]], off).wait_send()
    for c in range(4):
        x_copy(own_slot, c).wait_send()

    @pl.when(on_edge)
    def _():
        for c in range(4):
            h_copy(c).wait_send()

    for i in range(2):
        f_copy(i, core).wait_send()


def project_tokens(target, segment, bucket, mod_table, latents, w_query, w_key, w_value):
    vmem = pl.BlockSpec(memory_space=pltpu.VMEM)
    anywhere = pl.BlockSpec(memory_space=pl.ANY)
    dma = pltpu.SemaphoreType.DMA
    return pl.pallas_call(
        project_kernel,
        out_shape=(
            jax.ShapeDtypeStruct((2 * ROWS, 768), BF16),
            jax.ShapeDtypeStruct((3 * ROWS, 768), BF16),
            jax.ShapeDtypeStruct((3 * ROWS, 768), BF16),
            jax.ShapeDtypeStruct((8, 3 * ROWS), I32),
        ),
        in_specs=[vmem] * 5 + [anywhere] * 3,
        out_specs=(vmem,) * 4,
        scratch_shapes=[
            pltpu.VMEM((ROWS, BLOCK), BF16),
            pltpu.VMEM((ROWS, BLOCK), BF16),
            pltpu.VMEM((3, 4, 4, 4, 96, 384), BF16),
            pltpu.VMEM((3, ROWS, WIDTH), BF16),
            pltpu.VMEM((2, ROWS, 128), BF16),
            pltpu.VMEM((ROWS, 128), BF16),
            pltpu.VMEM((8, ROWS), I32),
            pltpu.VMEM((4, 8, ROWS), I32),
            dma((32,)), dma((32,)), dma((6, 3, 3)), dma((6, 3, 3)), dma((3,)), dma((3,)),
            dma((4,)), dma((4,)), dma((4,)), dma((2,)), dma((2,)), dma((2,)), dma((3,)),
        ],
        compiler_params=pltpu.CompilerParams(collective_id=0, has_side_effects=True, vmem_limit_bytes=60 * 2**20),
        name="project_tokens",
    )(target, segment, bucket, mod_table, latents, w_query, w_key, w_value)


Q_TILE, K_SPAN = 256, 1280


def attend_kernel(info, q, k, v, seg, out):
    tile = pl.program_id(1)
    base = info[0] * ROWS + tile * Q_TILE
    start = pl.multiple_of(jnp.clip(base - 512, 0, 3 * ROWS - K_SPAN), 128)
    span = pl.ds(start, K_SPAN)
    seg_keys = seg[0:1, span]
    seg_rows = seg[:, pl.ds(pl.multiple_of(base, 128), Q_TILE)]
    seg_query = jnp.transpose(seg_rows.astype(F32))[:, 0:1].astype(I32)
    scores = dot_nt(q[...], k[span]) * HEAD_DIM**-0.5
    scores = jnp.where(seg_query == seg_keys, scores, -1e30)
    weight = jnp.exp(scores - jnp.max(scores, axis=1, keepdims=True))
    total = jnp.sum(weight, axis=1, keepdims=True)
    out[...] = dot((weight / total).astype(BF16), v[span]).astype(BF16)


def attend(info, q, k, v, seg):
    return pl.pallas_call(
        attend_kernel,
        out_shape=jax.ShapeDtypeStruct((2 * ROWS, 768), BF16),
        grid_spec=pltpu.PrefetchScalarGridSpec(
            num_scalar_prefetch=1,
            grid=(6, 2 * ROWS // Q_TILE),
            in_specs=[
                pl.BlockSpec((Q_TILE, HEAD_DIM), lambda h, t, info: (t, h)),
                pl.BlockSpec((3 * ROWS, HEAD_DIM), lambda h, t, info: (0, h)),
                pl.BlockSpec((3 * ROWS, HEAD_DIM), lambda h, t, info: (0, h)),
                pl.BlockSpec((8, 3 * ROWS), lambda h, t, info: (0, 0)),
            ],
            out_specs=pl.BlockSpec((Q_TILE, HEAD_DIM), lambda h, t, info: (t, h)),
        ),
        name="attend",
    )(info, q, k, v, seg)


def exchange_kernel(o, out, landed, local, send, recv):
    me_dp, me_seq = lax.axis_index("dp"), lax.axis_index("seq")
    x_hi, core = me_seq // 2, me_seq % 2
    sibling = (me_dp, x_hi * 2 + (1 - core))
    barrier = pltpu.get_barrier_semaphore()
    pl.semaphore_signal(barrier, inc=1, device_id=sibling, device_id_type=MESH)
    pl.semaphore_wait(barrier, 1)
    there = pl.ds(pl.multiple_of((1 - core) * ROWS, ROWS), ROWS)
    here = pl.ds(pl.multiple_of(core * ROWS, ROWS), ROWS)
    copy = pltpu.make_async_remote_copy(
        src_ref=o.at[there], dst_ref=landed, send_sem=send, recv_sem=recv, device_id=sibling, device_id_type=MESH,
    )
    copy.start()
    for h in range(2):
        out[:, pl.ds(pl.multiple_of(h * 768 + core * 384, 128), 384)] = o[here, 384 * h : 384 * h + 384]
    copy.wait()
    for h in range(2):
        out[:, pl.ds(pl.multiple_of(h * 768 + (1 - core) * 384, 128), 384)] = landed[:, 384 * h : 384 * h + 384]


def exchange(o):
    vmem = pl.BlockSpec(memory_space=pltpu.VMEM)
    return pl.pallas_call(
        exchange_kernel,
        out_shape=jax.ShapeDtypeStruct((ROWS, 2 * 768), BF16),
        in_specs=[vmem],
        out_specs=vmem,
        scratch_shapes=[
            pltpu.VMEM((ROWS, 768), BF16), pltpu.SemaphoreType.DMA, pltpu.SemaphoreType.DMA, pltpu.SemaphoreType.DMA,
        ],
        compiler_params=pltpu.CompilerParams(collective_id=1, has_side_effects=True, vmem_limit_bytes=32 * 2**20),
        name="exchange_heads",
    )(o)


def on_device(latents, target, segment_ids, clip_bucket, mod_table, w_query, w_key, w_value):
    q, k, v, seg = project_tokens(
        target.reshape(1, ROWS), segment_ids, clip_bucket, mod_table, latents, w_query, w_key, w_value
    )
    info = (lax.axis_index("seq") // 2).astype(I32).reshape(1)
    return exchange(attend(info, q, k, v, seg))


def solution(mesh):
    in_specs = (
        P(("dp", "seq"), None),
        P(("dp", "seq")),
        P("dp", "seq"),
        P("dp", None),
        P(),
        P("dp", "seq"),
        P("dp", "seq"),
        P("dp", "seq"),
    )
    out_specs = P(("dp", "seq"), None)
    return jax.shard_map(on_device, mesh=mesh, in_specs=in_specs, out_specs=out_specs, check_vma=False)
```

```python
import functools

import jax
import jax.numpy as jnp
from jax import lax
from jax.experimental import pallas as pl
from jax.experimental.pallas import tpu as pltpu
from jax.sharding import PartitionSpec as P

MESH = pl.DeviceIdType.MESH
F32, BF16, I32 = jnp.float32, jnp.bfloat16, jnp.int32
ROWS, WIDTH, HALF, HEAD_DIM = 512, 3072, 1536, 128
BLOCK = WIDTH + HALF + 128
KEY, VALUE, QUERY = 0, 1, 2
Q_TILE, SPANS, LOG2E = 256, (640, 896, 1280), 1.4426950408889634
PARTS = (
    (KEY, 0, 48, (0, 1, 2)),
    (KEY, 48, 48, (0, 2, 1)),
    (VALUE, 0, 48, (0, 1, 2)),
    (VALUE, 48, 48, (0, 2, 1)),
    (QUERY, 0, 32, (1, 2, 0)),
    (QUERY, 32, 32, (0, 1, 2)),
    (QUERY, 64, 32, (0, 2, 1)),
)
FRONT = 2432


def dot(a, b):
    return jnp.dot(a, b, preferred_element_type=F32)


def dot_nt(a, b):
    return lax.dot_general(a, b, (((1,), (1,)), ((), ())), preferred_element_type=F32)


def iota(shape, dim):
    return lax.broadcasted_iota(I32, shape, dim)


def one_hot(row_ids, lane_ids):
    return jnp.where(row_ids == lane_ids, 1.0, 0.0).astype(BF16)


def project_kernel(
    target, segment, bucket, mod_table, latents_in, w_query, w_key, w_value,
    q_out, k_out, v_out, seg_out, info_out,
    latents, q_made, k_made, v_made, outgoing, front, back, incoming, weights, hidden, tags, hits, keys, seg_all,
    z_send, z_recv, p_send, p_recv, w_send, w_recv, s_send, s_recv, x_send, x_recv, h_send, h_recv, f_send, f_recv, o_send, o_recv, o_local, local,
):
    me_dp, me_seq = lax.axis_index("dp"), lax.axis_index("seq")
    x_lo, z, y = me_dp // 16, (me_dp // 4) % 4, me_dp % 4
    x_hi, core = me_seq // 2, me_seq % 2
    me = (x_hi * 2 + x_lo, z, y)
    sibling = (me_dp, x_hi * 2 + (1 - core))

    def at_chip(c):
        return ((c[0] % 2) * 16 + c[1] * 4 + c[2], (c[0] // 2) * 2 + core)

    def along_z(dz):
        return (x_lo * 16 + ((z + dz) % 4) * 4 + y, me_seq)

    def in_plane(b, sign):
        return (((x_lo + b // 4) % 2) * 16 + z * 4 + (y + 4 + sign * (b % 4)) % 4, me_seq)

    def seq_peer(r):
        if r == 1:
            return sibling
        return (me_dp, (1 - x_hi) * 2 + (core if r == 2 else 1 - core))

    barrier = pltpu.get_barrier_semaphore()

    def greet(k, carry):
        pl.semaphore_signal(barrier, inc=1, device_id=((me_dp + k) % 32, me_seq), device_id_type=MESH)
        return carry

    lax.fori_loop(1, 32, greet, 0)
    for peer in (seq_peer(1), seq_peer(2), seq_peer(3), ((1 - x_lo) * 16 + z * 4 + y, (1 - x_hi) * 2 + core)):
        pl.semaphore_signal(barrier, inc=1, device_id=peer, device_id_type=MESH)

    load = pltpu.make_async_copy(latents_in, latents, local.at[3])
    load.start()
    own = []
    for m, shard in ((KEY, w_key), (VALUE, w_value), (QUERY, w_query)):
        copy = pltpu.make_async_copy(shard, weights.at[m, me[0], z, y], local.at[m])
        copy.start()
        own.append(copy)
    seg_all[me_seq] = jnp.broadcast_to(segment[...], (8, ROWS))
    for copy in own:
        copy.wait()
    pl.semaphore_wait(barrier, 35)

    def w_copy(p, phase, pos, off):
        m, first_row, row_count, order = PARTS[p]
        axis, done = order[phase], order[:phase]
        index = [m]
        for ax in range(3):
            index.append(pos % 4 if ax == axis else slice(None) if ax in done else me[ax])
        index.append(pl.ds(first_row, row_count))
        there = list(me)
        there[axis] = (there[axis] + off) % 4
        piece = weights.at[tuple(index)]
        return pltpu.make_async_remote_copy(
            src_ref=piece, dst_ref=piece, send_sem=w_send.at[p, phase, off - 1], recv_sem=w_recv.at[p, phase, off - 1],
            device_id=at_chip(there), device_id_type=MESH,
        )

    def w_start(p, phase, offs=(1, 3, 2)):
        axis = PARTS[p][3][phase]
        for off in offs:
            w_copy(p, phase, me[axis], off).start()

    def w_arrived(p, phase):
        axis = PARTS[p][3][phase]
        for off in (1, 3, 2):
            w_copy(p, phase, me[axis] + 4 - off, off).wait_recv()

    for p in range(len(PARTS)):
        w_start(p, 0)

    def s_copy(r, slot):
        return pltpu.make_async_remote_copy(
            src_ref=seg_all.at[slot], dst_ref=seg_all.at[slot], send_sem=s_send.at[r - 1], recv_sem=s_recv.at[r - 1],
            device_id=seq_peer(r), device_id_type=MESH,
        )

    for r in (1, 2, 3):
        s_copy(r, me_seq).start()

    row = target[...] & (ROWS - 1)
    dest = target[...] >> 11
    block = ((((dest >> 2) & 3) + 4 - z) & 3) * 8 + (((dest >> 4) + x_lo) & 1) * 4 + (((dest & 3) + 4 - y) & 3)
    block_hit = jnp.where(iota((32, ROWS), 0) == block, 1.0, 0.0)
    before = one_hot(jnp.minimum(iota((ROWS, ROWS), 0) + 1, iota((ROWS, ROWS), 1)), iota((ROWS, ROWS), 0) + 1)
    earlier = dot(block_hit.astype(BF16), before)
    rank = jnp.sum(block_hit * earlier, axis=0, keepdims=True).astype(I32)
    late = rank >= 16
    keys[0:1] = jnp.where(late, -1, block * 16 + rank)
    keys[1:2] = jnp.where(late, block * 16 + rank - 16, -1)
    keys[2:3] = jnp.where(late, block * 16 + rank - 8, -1)
    token_bucket = jnp.zeros((1, ROWS), I32)
    for clip in range(8):
        token_bucket += jnp.where(segment[...] == clip, bucket[:, clip : clip + 1], 0)
    stacked = jnp.concatenate([row.astype(F32), token_bucket.astype(F32), jnp.zeros((6, ROWS), F32)], axis=0)
    columns = jnp.transpose(stacked)
    row_col, bucket_col = columns[:, 0:1], columns[:, 1:2]
    lane = iota((ROWS, 128), 1)
    hits[...] = jnp.where(bucket_col == lane.astype(F32), 1.0, 0.0).astype(BF16)
    high = jnp.where(row_col >= 256.0, 1.0, 0.0)
    low = row_col - 256.0 * high
    kind = lane % 3
    tag = jnp.where(kind == 0, low, jnp.where(kind == 1, high, 1.0))
    tags[0] = jnp.where(lane < 3, tag, 0.0).astype(BF16)
    tags[1] = jnp.where((lane >= 3) & (lane < 6), tag, 0.0).astype(BF16)

    fore, aft = pl.ds(0, FRONT), pl.ds(FRONT, BLOCK - FRONT)

    def z_copy(stage, dz, sign):
        if stage == 0:
            src, dst = outgoing.at[dz, :, :, fore], front.at[dz]
        else:
            src, dst = back.at[dz], incoming.at[dz, :, :, aft]
        return pltpu.make_async_remote_copy(
            src_ref=src, dst_ref=dst, send_sem=z_send.at[stage, dz], recv_sem=z_recv.at[stage, dz],
            device_id=along_z(dz if sign > 0 else 4 - dz), device_id_type=MESH,
        )

    def p_copy(stage, b, sign):
        if stage == 0:
            src, dst = outgoing.at[:, b, :, aft], back.at[:, b]
        else:
            src, dst = front.at[:, b], incoming.at[:, b, :, fore]
        return pltpu.make_async_remote_copy(
            src_ref=src, dst_ref=dst, send_sem=p_send.at[stage, b], recv_sem=p_recv.at[stage, b],
            device_id=in_plane(b, sign), device_id_type=MESH,
        )

    z_order, p_order = (1, 3, 2), (1, 4, 3, 5, 2, 7, 6)

    def stay(src, dst, i):
        copy = pltpu.make_async_copy(src, dst, local.at[i])
        copy.start()
        return copy

    def pack(c, carry):
        dz = (c + 1) % 4
        base = dz * 128
        ids = iota((128, ROWS), 0) + base
        first = one_hot(ids, keys[0:1])
        left = one_hot(ids, keys[1:2])
        right = one_hot(ids, keys[2:3])

        def put(lo, hi, value):
            outgoing[dz, :, :, lo:hi] = value.astype(BF16).reshape(8, 16, hi - lo)

        put(0, WIDTH, dot(first, latents[...]))
        put(WIDTH, WIDTH + HALF, dot(left, latents[:, 0:HALF]) + dot(right, latents[:, HALF:WIDTH]))
        put(WIDTH + HALF, BLOCK, dot(first, tags[0]) + dot(left + right, tags[1]))

        @pl.when(c < 3)
        def _():
            z_copy(0, dz, 1).start()

        return carry

    for p in range(len(PARTS)):
        w_arrived(p, 0)
        w_start(p, 1)
    load.wait()
    lax.fori_loop(0, 4, pack, 0)

    for b in p_order:
        p_copy(0, b, 1).start()
    stays = [stay(outgoing.at[0, :, :, fore], front.at[0], 0), stay(outgoing.at[:, 0, :, aft], back.at[:, 0], 1)]
    for r in (1, 2, 3):
        s_copy(r, (seq_peer(r)[1])).wait_recv()
    for i in range(3):
        seg_out[:, 512 * i : 512 * i + 512] = seg_all[x_hi + i]

    window = seg_out[0:1, :]
    info_lane = iota((1, 128), 1)
    for t in range(ROWS // Q_TILE):
        base = pl.multiple_of((x_hi + core) * ROWS + t * Q_TILE, 128)
        ids = seg_out[0:1, pl.ds(base, Q_TILE)]
        first = jnp.sum(jnp.where(window < ids[:, 0:1], 1, 0), axis=1, keepdims=True)
        last = jnp.sum(jnp.where(window <= ids[:, Q_TILE - 1 :], 1, 0), axis=1, keepdims=True)
        info_out[t : t + 1, :] = jnp.where(info_lane == 0, first, jnp.where(info_lane == 1, last, base))

    for copy in stays:
        copy.wait()
    for dz in z_order:
        z_copy(0, dz, -1).wait_recv()
    for b in p_order:
        p_copy(1, b, 1).start()
    for b in p_order:
        p_copy(0, b, -1).wait_recv()
    for dz in z_order:
        z_copy(1, dz, 1).start()
    stays = [stay(front.at[:, 0], incoming.at[:, 0, :, fore], 0), stay(back.at[0], incoming.at[0, :, :, aft], 1)]
    for p in (0, 1):
        w_arrived(p, 1)
        w_start(p, 2, (2,))
    for p in range(2, len(PARTS)):
        w_arrived(p, 1)
    for copy in stays:
        copy.wait()
    for dz in z_order:
        z_copy(1, dz, -1).wait_recv()
    for b in p_order:
        p_copy(1, b, -1).wait_recv()
    for p in (0, 1):
        w_start(p, 2, (1, 3))
        w_start(p + 2, 2, (2,))

    def received(lo, hi):
        return incoming[:, :, :, lo:hi].reshape(ROWS, hi - lo)

    own_slot, sib_slot, halo_slot = x_hi + core, x_hi + 1 - core, 2 - 2 * x_hi
    pick_lane = iota((8, 128), 1)
    pick_row = iota((8, 128), 0)
    pick_kind = pick_lane - 3 * pick_row
    pick = jnp.where(
        pick_row < 2,
        jnp.where(pick_kind == 0, 1.0, jnp.where(pick_kind == 1, 256.0, jnp.where(pick_kind == 2, 512.0, 0.0))),
        0.0,
    ).astype(BF16)
    rows_in = dot_nt(pick, received(WIDTH + HALF, BLOCK)).astype(I32) - 512
    odd = (iota((1, ROWS), 1) & 15) >= 8
    keys[0:1] = rows_in[0:1]
    keys[1:2] = jnp.where(odd, -1, rows_in[1:2])
    keys[2:3] = jnp.where(odd, rows_in[1:2], -1)

    def chunk(slot, c):
        return hidden.at[slot, pl.ds(pl.multiple_of(c * 128, 128), 128)]

    def x_copy(slot, c):
        return pltpu.make_async_remote_copy(
            src_ref=chunk(slot, c), dst_ref=chunk(slot, c), send_sem=x_send.at[c], recv_sem=x_recv.at[c],
            device_id=sibling, device_id_type=MESH,
        )

    def h_copy(c):
        return pltpu.make_async_remote_copy(
            src_ref=chunk(own_slot, c), dst_ref=chunk(2 * x_hi, c), send_sem=h_send.at[c], recv_sem=h_recv.at[c % 2],
            device_id=(me_dp, (1 - x_hi) * 2 + c // 2), device_id_type=MESH,
        )

    def f_copy(i, owner):
        c = 2 * owner + i
        return pltpu.make_async_remote_copy(
            src_ref=chunk(halo_slot, c), dst_ref=chunk(halo_slot, c), send_sem=f_send.at[i], recv_sem=f_recv.at[i],
            device_id=sibling, device_id_type=MESH,
        )

    on_edge = x_hi + core == 1

    def place(c, carry):
        base = pl.multiple_of(c * 128, 128)
        rows = pl.ds(base, 128)
        ids = iota((128, ROWS), 0) + base
        whole = dot(one_hot(ids, keys[0:1]), received(0, WIDTH))
        left = dot(one_hot(ids, keys[1:2]), received(WIDTH, WIDTH + HALF))
        right = dot(one_hot(ids, keys[2:3]), received(WIDTH, WIDTH + HALF))
        placed = whole + jnp.concatenate([left, right], axis=1)
        centered = placed - jnp.mean(placed, axis=1, keepdims=True)
        var = jnp.mean(centered * centered, axis=1, keepdims=True)
        normalized = centered * lax.rsqrt(var + 1e-6)
        modulation = dot(hits[rows, 0:16], mod_table[...])
        hidden[own_slot, rows] = (normalized * (1.0 + modulation[:, WIDTH:]) + modulation[:, :WIDTH]).astype(BF16)
        x_copy(own_slot, c).start()

        @pl.when(on_edge)
        def _():
            h_copy(c).start()

        return carry

    lax.fori_loop(0, 4, place, 0)

    made, outs = (k_made, v_made, q_made), (k_out, v_out, q_out)

    def project(m, slot, at):
        def step(r, carry):
            w = jnp.concatenate([weights[m, 2 * h : 2 * h + 2].reshape(WIDTH, 384) for h in range(2)], axis=1)
            rows = pl.ds(pl.multiple_of(r * 256, 256), 256)
            result = dot(hidden[slot, rows], w).astype(BF16)
            for h in range(2):
                made[m][h, pl.ds(pl.multiple_of(at * ROWS + r * 256, 256), 256)] = result[:, 384 * h : 384 * h + 384]
            return carry

        lax.fori_loop(0, 2, step, 0)

    def o_there(m, at, to, owner):
        return pltpu.make_async_remote_copy(
            src_ref=made[m].at[:, pl.ds(pl.multiple_of(at * ROWS, ROWS), ROWS)],
            dst_ref=outs[m].at[owner, :, pl.ds(pl.multiple_of(to * ROWS, ROWS), ROWS)],
            send_sem=o_send.at[m, to], recv_sem=o_recv.at[m, to], device_id=sibling, device_id_type=MESH,
        )

    def o_here(m, at, to):
        return pltpu.make_async_copy(
            made[m].at[:, pl.ds(pl.multiple_of(at * ROWS, ROWS), ROWS)],
            outs[m].at[core, :, pl.ds(pl.multiple_of(to * ROWS, ROWS), ROWS)],
            o_local.at[m, to],
        )

    def make(m, slot):
        project(m, slot, slot)
        o_there(m, slot, slot, core).start()
        o_here(m, slot, slot).start()

    for p in (0, 1):
        w_arrived(p, 2)
        w_start(p + 2, 2, (1, 3))
    for p in (4, 5, 6):
        w_start(p, 2, (2,))
    make(KEY, own_slot)
    for c in range(4):
        x_copy(sib_slot, c).wait_recv()
    make(KEY, sib_slot)
    for p in (2, 3):
        w_arrived(p, 2)
    for p in (4, 5, 6):
        w_start(p, 2, (1, 3))
    make(VALUE, own_slot)
    make(VALUE, sib_slot)
    for i in range(2):
        h_copy(2 * core + i).wait_recv()
        f_copy(i, core).start()
    for i in range(2):
        f_copy(i, 1 - core).wait_recv()
    make(KEY, halo_slot)
    make(VALUE, halo_slot)
    for p in (4, 5, 6):
        w_arrived(p, 2)
    project(QUERY, sib_slot, 1)
    o_there(QUERY, 1, 0, core).start()
    project(QUERY, own_slot, 0)
    o_here(QUERY, 0, 0).start()

    for m in (KEY, VALUE):
        for slot in range(3):
            o_here(m, slot, slot).wait()
            o_there(m, slot, slot, core).wait_send()
            o_there(m, slot, slot, 1 - core).wait_recv()
    o_here(QUERY, 0, 0).wait()
    o_there(QUERY, 1, 0, core).wait_send()
    o_there(QUERY, 1, 0, 1 - core).wait_recv()

    for r in (1, 2, 3):
        s_copy(r, me_seq).wait_send()
    for stage in (0, 1):
        for dz in z_order:
            z_copy(stage, dz, 1).wait_send()
        for b in p_order:
            p_copy(stage, b, 1).wait_send()
    for p in range(len(PARTS)):
        for phase in range(3):
            for off in (1, 3, 2):
                w_copy(p, phase, me[PARTS[p][3][phase]], off).wait_send()
    for c in range(4):
        x_copy(own_slot, c).wait_send()

    @pl.when(on_edge)
    def _():
        for c in range(4):
            h_copy(c).wait_send()

    for i in range(2):
        f_copy(i, core).wait_send()


def project_tokens(target, segment, bucket, mod_table, latents_in, w_query, w_key, w_value):
    vmem = pl.BlockSpec(memory_space=pltpu.VMEM)
    anywhere = pl.BlockSpec(memory_space=pl.ANY)
    dma = pltpu.SemaphoreType.DMA
    return pl.pallas_call(
        project_kernel,
        out_shape=(
            jax.ShapeDtypeStruct((2, 2, ROWS, 384), BF16),
            jax.ShapeDtypeStruct((2, 2, 3 * ROWS, 384), BF16),
            jax.ShapeDtypeStruct((2, 2, 3 * ROWS, 384), BF16),
            jax.ShapeDtypeStruct((8, 3 * ROWS), I32),
            jax.ShapeDtypeStruct((ROWS // Q_TILE, 128), I32),
        ),
        in_specs=[vmem] * 4 + [anywhere] * 4,
        out_specs=(anywhere,) * 3 + (vmem,) * 2,
        scratch_shapes=[
            pltpu.VMEM((ROWS, WIDTH), BF16),
            pltpu.VMEM((2, 2 * ROWS, 384), BF16),
            pltpu.VMEM((2, 3 * ROWS, 384), BF16),
            pltpu.VMEM((2, 3 * ROWS, 384), BF16),
            pltpu.VMEM((4, 8, 16, BLOCK), BF16),
            pltpu.VMEM((4, 8, 16, FRONT), BF16),
            pltpu.VMEM((4, 8, 16, BLOCK - FRONT), BF16),
            pltpu.VMEM((4, 8, 16, BLOCK), BF16),
            pltpu.VMEM((3, 4, 4, 4, 96, 384), BF16),
            pltpu.VMEM((3, ROWS, WIDTH), BF16),
            pltpu.VMEM((2, ROWS, 128), BF16),
            pltpu.VMEM((ROWS, 128), BF16),
            pltpu.VMEM((8, ROWS), I32),
            pltpu.VMEM((4, 8, ROWS), I32),
            dma((2, 4)), dma((2, 4)), dma((2, 8)), dma((2, 8)), dma((len(PARTS), 3, 3)), dma((len(PARTS), 3, 3)), dma((3,)), dma((3,)),
            dma((4,)), dma((4,)), dma((4,)), dma((2,)), dma((2,)), dma((2,)), dma((3, 3)), dma((3, 3)), dma((3, 3)), dma((4,)),
        ],
        compiler_params=pltpu.CompilerParams(collective_id=0, has_side_effects=True, vmem_limit_bytes=60 * 2**20),
        name="project_tokens",
    )(target, segment, bucket, mod_table, latents_in, w_query, w_key, w_value)


def attend_kernel(info, q, k, v, seg, out):
    tile = pl.program_id(1)
    begin = (info[tile, 0] // 128) * 128
    span = info[tile, 1] - begin
    base = pl.multiple_of(info[tile, 2], 128)
    seg_query = jnp.transpose(seg[:, pl.ds(base, Q_TILE)].astype(F32))[:, 0:1]

    def over(width):
        start = pl.multiple_of(jnp.minimum(begin, 3 * ROWS - width), 128)
        rows = pl.ds(start, width)
        bias = jnp.where(seg_query == seg[0:1, rows].astype(F32), 0.0, -1e30)
        ones = jnp.ones((width, HEAD_DIM), BF16)
        for h in range(3):
            cols = slice(h * HEAD_DIM, (h + 1) * HEAD_DIM)
            scores = dot_nt(q[0, 0, :, cols], k[0, 0, rows, cols]) + bias
            weight = jnp.exp2((scores - jnp.max(scores, axis=1, keepdims=True)) * (HEAD_DIM**-0.5 * LOG2E))
            mixed = dot(weight.astype(BF16), jnp.concatenate([v[0, 0, rows, cols], ones], axis=1))
            out[:, cols] = (mixed[:, :HEAD_DIM] / mixed[:, HEAD_DIM:]).astype(BF16)

    least = -1
    for width in SPANS:
        pl.when((span > least) & (span <= width))(functools.partial(over, width))
        least = width


def attend(info, q, k, v, seg):
    return pl.pallas_call(
        attend_kernel,
        out_shape=jax.ShapeDtypeStruct((ROWS, 1536), BF16),
        grid_spec=pltpu.PrefetchScalarGridSpec(
            num_scalar_prefetch=1,
            grid=(4, ROWS // Q_TILE),
            in_specs=[
                pl.BlockSpec((1, 1, Q_TILE, 384), lambda g, t, info: (g % 2, g // 2, t, 0)),
                pl.BlockSpec((1, 1, 3 * ROWS, 384), lambda g, t, info: (g % 2, g // 2, 0, 0)),
                pl.BlockSpec((1, 1, 3 * ROWS, 384), lambda g, t, info: (g % 2, g // 2, 0, 0)),
                pl.BlockSpec((8, 3 * ROWS), lambda g, t, info: (0, 0)),
            ],
            out_specs=pl.BlockSpec((Q_TILE, 384), lambda g, t, info: (t, g)),
        ),
        compiler_params=pltpu.CompilerParams(vmem_limit_bytes=60 * 2**20),
        name="attend",
    )(info, q, k, v, seg)


def on_device(latents, target, segment_ids, clip_bucket, mod_table, w_query, w_key, w_value):
    q, k, v, seg, info = project_tokens(
        target.reshape(1, ROWS), segment_ids, clip_bucket, mod_table, latents, w_query, w_key, w_value
    )
    return attend(info, q, k, v, seg)


def solution(mesh):
    in_specs = (
        P(("dp", "seq"), None),
        P(("dp", "seq")),
        P("dp", "seq"),
        P("dp", None),
        P(),
        P("dp", "seq"),
        P("dp", "seq"),
        P("dp", "seq"),
    )
    out_specs = P(("dp", "seq"), None)
    return jax.shard_map(on_device, mesh=mesh, in_specs=in_specs, out_specs=out_specs, check_vma=False)
```

```python
import functools

import jax
import jax.numpy as jnp
from jax import lax
from jax.experimental import pallas as pl
from jax.experimental.pallas import tpu as pltpu
from jax.sharding import PartitionSpec as P

MESH = pl.DeviceIdType.MESH
F32, BF16, I32 = jnp.float32, jnp.bfloat16, jnp.int32
ROWS, WIDTH, HALF, HEAD_DIM = 512, 3072, 1536, 128
BLOCK = WIDTH + HALF + 128
KEY, VALUE, QUERY = 0, 1, 2
Q_TILE, SPANS, LOG2E = 256, (512, 640, 768, 896, 1024, 1280), 1.4426950408889634
PARTS = (
    (KEY, 0, 48, (0, 1, 2)),
    (KEY, 48, 48, (0, 2, 1)),
    (VALUE, 0, 48, (0, 1, 2)),
    (VALUE, 48, 48, (0, 2, 1)),
    (QUERY, 0, 48, (1, 2, 0)),
    (QUERY, 48, 32, (0, 1, 2)),
    (QUERY, 80, 16, (0, 2, 1)),
)
FRONT = 2432


def dot(a, b):
    return jnp.dot(a, b, preferred_element_type=F32)


def dot_nt(a, b):
    return lax.dot_general(a, b, (((1,), (1,)), ((), ())), preferred_element_type=F32)


def iota(shape, dim):
    return lax.broadcasted_iota(I32, shape, dim)


def one_hot(row_ids, lane_ids):
    return jnp.where(row_ids == lane_ids, 1.0, 0.0).astype(BF16)


def project_kernel(
    target, segment, bucket, mod_table, latents_in, w_query, w_key, w_value,
    q_out, k_out, v_out, seg_out, info_out,
    latents, q_made, k_made, v_made, outgoing, front, back, incoming, weights, hidden, tags, hits, keys, seg_all,
    z_send, z_recv, p_send, p_recv, w_send, w_recv, s_send, s_recv, x_send, x_recv, h_send, h_recv, f_send, f_recv, o_send, o_recv, o_local, local,
):
    me_dp, me_seq = lax.axis_index("dp"), lax.axis_index("seq")
    x_lo, z, y = me_dp // 16, (me_dp // 4) % 4, me_dp % 4
    x_hi, core = me_seq // 2, me_seq % 2
    me = (x_hi * 2 + x_lo, z, y)
    sibling = (me_dp, x_hi * 2 + (1 - core))

    def at_chip(c):
        return ((c[0] % 2) * 16 + c[1] * 4 + c[2], (c[0] // 2) * 2 + core)

    def along_z(dz):
        return (x_lo * 16 + ((z + dz) % 4) * 4 + y, me_seq)

    def in_plane(b, sign):
        return (((x_lo + b // 4) % 2) * 16 + z * 4 + (y + 4 + sign * (b % 4)) % 4, me_seq)

    def seq_peer(r):
        if r == 1:
            return sibling
        return (me_dp, (1 - x_hi) * 2 + (core if r == 2 else 1 - core))

    barrier = pltpu.get_barrier_semaphore()

    def greet(k, carry):
        pl.semaphore_signal(barrier, inc=1, device_id=((me_dp + k) % 32, me_seq), device_id_type=MESH)
        return carry

    lax.fori_loop(1, 32, greet, 0)
    for peer in (seq_peer(1), seq_peer(2), seq_peer(3), ((1 - x_lo) * 16 + z * 4 + y, (1 - x_hi) * 2 + core)):
        pl.semaphore_signal(barrier, inc=1, device_id=peer, device_id_type=MESH)

    load = pltpu.make_async_copy(latents_in, latents, local.at[3])
    load.start()
    own = []
    for m, shard in ((KEY, w_key), (VALUE, w_value), (QUERY, w_query)):
        copy = pltpu.make_async_copy(shard, weights.at[m, me[0], z, y], local.at[m])
        copy.start()
        own.append(copy)
    seg_all[me_seq] = jnp.broadcast_to(segment[...], (8, ROWS))
    for copy in own:
        copy.wait()
    pl.semaphore_wait(barrier, 35)

    def w_copy(p, phase, pos, off):
        m, first_row, row_count, order = PARTS[p]
        axis, done = order[phase], order[:phase]
        index = [m]
        for ax in range(3):
            index.append(pos % 4 if ax == axis else slice(None) if ax in done else me[ax])
        index.append(pl.ds(first_row, row_count))
        there = list(me)
        there[axis] = (there[axis] + off) % 4
        piece = weights.at[tuple(index)]
        return pltpu.make_async_remote_copy(
            src_ref=piece, dst_ref=piece, send_sem=w_send.at[p, phase, off - 1], recv_sem=w_recv.at[p, phase, off - 1],
            device_id=at_chip(there), device_id_type=MESH,
        )

    def w_start(p, phase, offs=(1, 3, 2)):
        axis = PARTS[p][3][phase]
        for off in offs:
            w_copy(p, phase, me[axis], off).start()

    def w_arrived(p, phase):
        axis = PARTS[p][3][phase]
        for off in (1, 3, 2):
            w_copy(p, phase, me[axis] + 4 - off, off).wait_recv()

    for p in range(len(PARTS)):
        w_start(p, 0)

    def s_copy(r, slot):
        return pltpu.make_async_remote_copy(
            src_ref=seg_all.at[slot], dst_ref=seg_all.at[slot], send_sem=s_send.at[r - 1], recv_sem=s_recv.at[r - 1],
            device_id=seq_peer(r), device_id_type=MESH,
        )

    for r in (1, 2, 3):
        s_copy(r, me_seq).start()

    row = target[...] & (ROWS - 1)
    dest = target[...] >> 11
    block = ((((dest >> 2) & 3) + 4 - z) & 3) * 8 + (((dest >> 4) + x_lo) & 1) * 4 + (((dest & 3) + 4 - y) & 3)
    block_hit = jnp.where(iota((32, ROWS), 0) == block, 1.0, 0.0)
    before = one_hot(jnp.minimum(iota((ROWS, ROWS), 0) + 1, iota((ROWS, ROWS), 1)), iota((ROWS, ROWS), 0) + 1)
    earlier = dot(block_hit.astype(BF16), before)
    rank = jnp.sum(block_hit * earlier, axis=0, keepdims=True).astype(I32)
    late = rank >= 16
    keys[0:1] = jnp.where(late, -1, block * 16 + rank)
    keys[1:2] = jnp.where(late, block * 16 + rank - 16, -1)
    keys[2:3] = jnp.where(late, block * 16 + rank - 8, -1)
    token_bucket = jnp.zeros((1, ROWS), I32)
    for clip in range(8):
        token_bucket += jnp.where(segment[...] == clip, bucket[:, clip : clip + 1], 0)
    stacked = jnp.concatenate([row.astype(F32), token_bucket.astype(F32), jnp.zeros((6, ROWS), F32)], axis=0)
    columns = jnp.transpose(stacked)
    row_col, bucket_col = columns[:, 0:1], columns[:, 1:2]
    lane = iota((ROWS, 128), 1)
    hits[...] = jnp.where(bucket_col == lane.astype(F32), 1.0, 0.0).astype(BF16)
    high = jnp.where(row_col >= 256.0, 1.0, 0.0)
    low = row_col - 256.0 * high
    kind = lane % 3
    tag = jnp.where(kind == 0, low, jnp.where(kind == 1, high, 1.0))
    tags[0] = jnp.where(lane < 3, tag, 0.0).astype(BF16)
    tags[1] = jnp.where((lane >= 3) & (lane < 6), tag, 0.0).astype(BF16)

    fore, aft = pl.ds(0, FRONT), pl.ds(FRONT, BLOCK - FRONT)

    def z_copy(stage, dz, sign):
        if stage == 0:
            src, dst = outgoing.at[dz, :, :, fore], front.at[dz]
        else:
            src, dst = back.at[dz], incoming.at[dz, :, :, aft]
        return pltpu.make_async_remote_copy(
            src_ref=src, dst_ref=dst, send_sem=z_send.at[stage, dz], recv_sem=z_recv.at[stage, dz],
            device_id=along_z(dz if sign > 0 else 4 - dz), device_id_type=MESH,
        )

    def p_copy(stage, b, sign):
        if stage == 0:
            src, dst = outgoing.at[:, b, :, aft], back.at[:, b]
        else:
            src, dst = front.at[:, b], incoming.at[:, b, :, fore]
        return pltpu.make_async_remote_copy(
            src_ref=src, dst_ref=dst, send_sem=p_send.at[stage, b], recv_sem=p_recv.at[stage, b],
            device_id=in_plane(b, sign), device_id_type=MESH,
        )

    z_order, p_order = (1, 3, 2), (1, 4, 3, 5, 2, 7, 6)

    def stay(src, dst, i):
        copy = pltpu.make_async_copy(src, dst, local.at[i])
        copy.start()
        return copy

    def pack(c, carry):
        dz = (c + 1) % 4
        base = dz * 128
        ids = iota((128, ROWS), 0) + base
        first = one_hot(ids, keys[0:1])
        left = one_hot(ids, keys[1:2])
        right = one_hot(ids, keys[2:3])

        def put(lo, hi, value):
            outgoing[dz, :, :, lo:hi] = value.astype(BF16).reshape(8, 16, hi - lo)

        put(0, WIDTH, dot(first, latents[...]))
        put(WIDTH, WIDTH + HALF, dot(left, latents[:, 0:HALF]) + dot(right, latents[:, HALF:WIDTH]))
        put(WIDTH + HALF, BLOCK, dot(first, tags[0]) + dot(left + right, tags[1]))

        @pl.when(c < 3)
        def _():
            z_copy(0, dz, 1).start()

        return carry

    for p in range(len(PARTS)):
        w_arrived(p, 0)
        w_start(p, 1)
    load.wait()
    lax.fori_loop(0, 4, pack, 0)

    for b in p_order:
        p_copy(0, b, 1).start()
    stays = [stay(outgoing.at[0, :, :, fore], front.at[0], 0), stay(outgoing.at[:, 0, :, aft], back.at[:, 0], 1)]
    for r in (1, 2, 3):
        s_copy(r, (seq_peer(r)[1])).wait_recv()
    for i in range(3):
        seg_out[:, 512 * i : 512 * i + 512] = seg_all[x_hi + i]

    window = seg_out[0:1, :]
    info_lane = iota((1, 128), 1)
    for t in range(ROWS // Q_TILE):
        base = pl.multiple_of((x_hi + core) * ROWS + t * Q_TILE, 128)
        ids = seg_out[0:1, pl.ds(base, Q_TILE)]
        first = jnp.sum(jnp.where(window < ids[:, 0:1], 1, 0), axis=1, keepdims=True)
        last = jnp.sum(jnp.where(window <= ids[:, Q_TILE - 1 :], 1, 0), axis=1, keepdims=True)
        info_out[t : t + 1, :] = jnp.where(info_lane == 0, first, jnp.where(info_lane == 1, last, base))

    for copy in stays:
        copy.wait()
    for dz in z_order:
        z_copy(0, dz, -1).wait_recv()
    for b in p_order:
        p_copy(1, b, 1).start()
    for b in p_order:
        p_copy(0, b, -1).wait_recv()
    for dz in z_order:
        z_copy(1, dz, 1).start()
    stays = [stay(front.at[:, 0], incoming.at[:, 0, :, fore], 0), stay(back.at[0], incoming.at[0, :, :, aft], 1)]
    for p in (0, 1):
        w_arrived(p, 1)
        w_start(p, 2, (2,))
    for p in range(2, len(PARTS)):
        w_arrived(p, 1)
    for copy in stays:
        copy.wait()
    for dz in z_order:
        z_copy(1, dz, -1).wait_recv()
    for b in p_order:
        p_copy(1, b, -1).wait_recv()
    for p in (0, 1):
        w_start(p, 2, (1, 3))
        w_start(p + 2, 2, (2,))
    w_start(4, 2)

    def received(lo, hi):
        return incoming[:, :, :, lo:hi].reshape(ROWS, hi - lo)

    own_slot, sib_slot, halo_slot = x_hi + core, x_hi + 1 - core, 2 - 2 * x_hi
    pick_lane = iota((8, 128), 1)
    pick_row = iota((8, 128), 0)
    pick_kind = pick_lane - 3 * pick_row
    pick = jnp.where(
        pick_row < 2,
        jnp.where(pick_kind == 0, 1.0, jnp.where(pick_kind == 1, 256.0, jnp.where(pick_kind == 2, 512.0, 0.0))),
        0.0,
    ).astype(BF16)
    rows_in = dot_nt(pick, received(WIDTH + HALF, BLOCK)).astype(I32) - 512
    odd = (iota((1, ROWS), 1) & 15) >= 8
    keys[0:1] = rows_in[0:1]
    keys[1:2] = jnp.where(odd, -1, rows_in[1:2])
    keys[2:3] = jnp.where(odd, rows_in[1:2], -1)

    def chunk(slot, c):
        return hidden.at[slot, pl.ds(pl.multiple_of(c * 128, 128), 128)]

    def x_copy(slot, c):
        return pltpu.make_async_remote_copy(
            src_ref=chunk(slot, c), dst_ref=chunk(slot, c), send_sem=x_send.at[c], recv_sem=x_recv.at[c],
            device_id=sibling, device_id_type=MESH,
        )

    def h_copy(c):
        return pltpu.make_async_remote_copy(
            src_ref=chunk(own_slot, c), dst_ref=chunk(2 * x_hi, c), send_sem=h_send.at[c], recv_sem=h_recv.at[c % 2],
            device_id=(me_dp, (1 - x_hi) * 2 + c // 2), device_id_type=MESH,
        )

    def f_copy(i, owner):
        c = 2 * owner + i
        return pltpu.make_async_remote_copy(
            src_ref=chunk(halo_slot, c), dst_ref=chunk(halo_slot, c), send_sem=f_send.at[i], recv_sem=f_recv.at[i],
            device_id=sibling, device_id_type=MESH,
        )

    on_edge = x_hi + core == 1

    def place(c, carry):
        base = pl.multiple_of(c * 128, 128)
        rows = pl.ds(base, 128)
        ids = iota((128, ROWS), 0) + base
        whole = dot(one_hot(ids, keys[0:1]), received(0, WIDTH))
        left = dot(one_hot(ids, keys[1:2]), received(WIDTH, WIDTH + HALF))
        right = dot(one_hot(ids, keys[2:3]), received(WIDTH, WIDTH + HALF))
        placed = whole + jnp.concatenate([left, right], axis=1)
        centered = placed - jnp.mean(placed, axis=1, keepdims=True)
        var = jnp.mean(centered * centered, axis=1, keepdims=True)
        normalized = centered * lax.rsqrt(var + 1e-6)
        modulation = dot(hits[rows, 0:16], mod_table[...])
        hidden[own_slot, rows] = (normalized * (1.0 + modulation[:, WIDTH:]) + modulation[:, :WIDTH]).astype(BF16)
        x_copy(own_slot, c).start()

        @pl.when(on_edge)
        def _():
            h_copy(c).start()

        return carry

    lax.fori_loop(0, 4, place, 0)

    made, outs = (k_made, v_made, q_made), (k_out, v_out, q_out)

    def project(m, slot, at):
        def step(r, carry):
            w = jnp.concatenate([weights[m, 2 * h : 2 * h + 2].reshape(WIDTH, 384) for h in range(2)], axis=1)
            rows = pl.ds(pl.multiple_of(r * 256, 256), 256)
            result = dot(hidden[slot, rows], w).astype(BF16)
            for h in range(2):
                made[m][h, pl.ds(pl.multiple_of(at * ROWS + r * 256, 256), 256)] = result[:, 384 * h : 384 * h + 384]
            return carry

        lax.fori_loop(0, 2, step, 0)

    def o_there(m, at, to, owner):
        return pltpu.make_async_remote_copy(
            src_ref=made[m].at[:, pl.ds(pl.multiple_of(at * ROWS, ROWS), ROWS)],
            dst_ref=outs[m].at[owner, :, pl.ds(pl.multiple_of(to * ROWS, ROWS), ROWS)],
            send_sem=o_send.at[m, to], recv_sem=o_recv.at[m, to], device_id=sibling, device_id_type=MESH,
        )

    def o_here(m, at, to):
        return pltpu.make_async_copy(
            made[m].at[:, pl.ds(pl.multiple_of(at * ROWS, ROWS), ROWS)],
            outs[m].at[core, :, pl.ds(pl.multiple_of(to * ROWS, ROWS), ROWS)],
            o_local.at[m, to],
        )

    def make(m, slot):
        project(m, slot, slot)
        o_there(m, slot, slot, core).start()
        o_here(m, slot, slot).start()

    for p in (0, 1):
        w_arrived(p, 2)
        w_start(p + 2, 2, (1, 3))
    for p in (5, 6):
        w_start(p, 2, (2,))
    make(KEY, own_slot)
    for c in range(4):
        x_copy(sib_slot, c).wait_recv()
    make(KEY, sib_slot)
    for p in (2, 3):
        w_arrived(p, 2)
    for p in (5, 6):
        w_start(p, 2, (1, 3))
    make(VALUE, own_slot)
    make(VALUE, sib_slot)
    for i in range(2):
        h_copy(2 * core + i).wait_recv()
        f_copy(i, core).start()
    for i in range(2):
        f_copy(i, 1 - core).wait_recv()
    make(KEY, halo_slot)
    make(VALUE, halo_slot)
    for p in (4, 5, 6):
        w_arrived(p, 2)
    project(QUERY, sib_slot, 1)
    o_there(QUERY, 1, 0, core).start()
    project(QUERY, own_slot, 0)
    o_here(QUERY, 0, 0).start()

    for m in (KEY, VALUE):
        for slot in range(3):
            o_here(m, slot, slot).wait()
            o_there(m, slot, slot, core).wait_send()
            o_there(m, slot, slot, 1 - core).wait_recv()
    o_here(QUERY, 0, 0).wait()
    o_there(QUERY, 1, 0, core).wait_send()
    o_there(QUERY, 1, 0, 1 - core).wait_recv()

    for r in (1, 2, 3):
        s_copy(r, me_seq).wait_send()
    for stage in (0, 1):
        for dz in z_order:
            z_copy(stage, dz, 1).wait_send()
        for b in p_order:
            p_copy(stage, b, 1).wait_send()
    for p in range(len(PARTS)):
        for phase in range(3):
            for off in (1, 3, 2):
                w_copy(p, phase, me[PARTS[p][3][phase]], off).wait_send()
    for c in range(4):
        x_copy(own_slot, c).wait_send()

    @pl.when(on_edge)
    def _():
        for c in range(4):
            h_copy(c).wait_send()

    for i in range(2):
        f_copy(i, core).wait_send()


def project_tokens(target, segment, bucket, mod_table, latents_in, w_query, w_key, w_value):
    vmem = pl.BlockSpec(memory_space=pltpu.VMEM)
    anywhere = pl.BlockSpec(memory_space=pl.ANY)
    dma = pltpu.SemaphoreType.DMA
    return pl.pallas_call(
        project_kernel,
        out_shape=(
            jax.ShapeDtypeStruct((2, 2, ROWS, 384), BF16),
            jax.ShapeDtypeStruct((2, 2, 3 * ROWS, 384), BF16),
            jax.ShapeDtypeStruct((2, 2, 3 * ROWS, 384), BF16),
            jax.ShapeDtypeStruct((8, 3 * ROWS), I32),
            jax.ShapeDtypeStruct((ROWS // Q_TILE, 128), I32),
        ),
        in_specs=[vmem] * 4 + [anywhere] * 4,
        out_specs=(anywhere,) * 3 + (vmem,) * 2,
        scratch_shapes=[
            pltpu.VMEM((ROWS, WIDTH), BF16),
            pltpu.VMEM((2, 2 * ROWS, 384), BF16),
            pltpu.VMEM((2, 3 * ROWS, 384), BF16),
            pltpu.VMEM((2, 3 * ROWS, 384), BF16),
            pltpu.VMEM((4, 8, 16, BLOCK), BF16),
            pltpu.VMEM((4, 8, 16, FRONT), BF16),
            pltpu.VMEM((4, 8, 16, BLOCK - FRONT), BF16),
            pltpu.VMEM((4, 8, 16, BLOCK), BF16),
            pltpu.VMEM((3, 4, 4, 4, 96, 384), BF16),
            pltpu.VMEM((3, ROWS, WIDTH), BF16),
            pltpu.VMEM((2, ROWS, 128), BF16),
            pltpu.VMEM((ROWS, 128), BF16),
            pltpu.VMEM((8, ROWS), I32),
            pltpu.VMEM((4, 8, ROWS), I32),
            dma((2, 4)), dma((2, 4)), dma((2, 8)), dma((2, 8)), dma((len(PARTS), 3, 3)), dma((len(PARTS), 3, 3)), dma((3,)), dma((3,)),
            dma((4,)), dma((4,)), dma((4,)), dma((2,)), dma((2,)), dma((2,)), dma((3, 3)), dma((3, 3)), dma((3, 3)), dma((4,)),
        ],
        compiler_params=pltpu.CompilerParams(collective_id=0, has_side_effects=True, vmem_limit_bytes=60 * 2**20),
        name="project_tokens",
    )(target, segment, bucket, mod_table, latents_in, w_query, w_key, w_value)


def attend_kernel(info, q, k, v, seg, out):
    tile = pl.program_id(1)
    begin = (info[tile, 0] // 128) * 128
    span = info[tile, 1] - begin
    base = pl.multiple_of(info[tile, 2], 128)
    seg_query = jnp.transpose(seg[:, pl.ds(base, Q_TILE)].astype(F32))[:, 0:1]

    def over(width):
        start = pl.multiple_of(jnp.minimum(begin, 3 * ROWS - width), 128)
        rows = pl.ds(start, width)
        bias = jnp.where(seg_query == seg[0:1, rows].astype(F32), 0.0, -1e30)
        ones = jnp.ones((width, HEAD_DIM), BF16)
        heads = [(g, slice(e * HEAD_DIM, (e + 1) * HEAD_DIM)) for g in range(2) for e in range(3)]

        def score(g, cols):
            return dot_nt(q[g, 0, :, cols], k[g, 0, rows, cols]) + bias

        ready = score(*heads[0])
        for i, (g, cols) in enumerate(heads):
            scores = ready
            if i + 1 < len(heads):
                ready = score(*heads[i + 1])
            weight = jnp.exp2((scores - jnp.max(scores, axis=1, keepdims=True)) * (HEAD_DIM**-0.5 * LOG2E))
            mixed = dot(weight.astype(BF16), jnp.concatenate([v[g, 0, rows, cols], ones], axis=1))
            out[:, g * 384 + cols.start : g * 384 + cols.stop] = (mixed[:, :HEAD_DIM] / mixed[:, HEAD_DIM:]).astype(BF16)

    least = -1
    for width in SPANS:
        pl.when((span > least) & (span <= width))(functools.partial(over, width))
        least = width


def attend(info, q, k, v, seg):
    return pl.pallas_call(
        attend_kernel,
        out_shape=jax.ShapeDtypeStruct((ROWS, 1536), BF16),
        grid_spec=pltpu.PrefetchScalarGridSpec(
            num_scalar_prefetch=1,
            grid=(2, ROWS // Q_TILE),
            in_specs=[
                pl.BlockSpec((2, 1, Q_TILE, 384), lambda h, t, info: (0, h, t, 0)),
                pl.BlockSpec((2, 1, 3 * ROWS, 384), lambda h, t, info: (0, h, 0, 0)),
                pl.BlockSpec((2, 1, 3 * ROWS, 384), lambda h, t, info: (0, h, 0, 0)),
                pl.BlockSpec((8, 3 * ROWS), lambda h, t, info: (0, 0)),
            ],
            out_specs=pl.BlockSpec((Q_TILE, 768), lambda h, t, info: (t, h)),
        ),
        compiler_params=pltpu.CompilerParams(vmem_limit_bytes=60 * 2**20),
        name="attend",
    )(info, q, k, v, seg)


def on_device(latents, target, segment_ids, clip_bucket, mod_table, w_query, w_key, w_value):
    q, k, v, seg, info = project_tokens(
        target.reshape(1, ROWS), segment_ids, clip_bucket, mod_table, latents, w_query, w_key, w_value
    )
    return attend(info, q, k, v, seg)


def solution(mesh):
    in_specs = (
        P(("dp", "seq"), None),
        P(("dp", "seq")),
        P("dp", "seq"),
        P("dp", None),
        P(),
        P("dp", "seq"),
        P("dp", "seq"),
        P("dp", "seq"),
    )
    out_specs = P(("dp", "seq"), None)
    return jax.shard_map(on_device, mesh=mesh, in_specs=in_specs, out_specs=out_specs, check_vma=False)
```

```python
import functools

import jax
import jax.numpy as jnp
from jax import lax
from jax.experimental import pallas as pl
from jax.experimental.pallas import tpu as pltpu
from jax.sharding import PartitionSpec as P

MESH = pl.DeviceIdType.MESH
F32, BF16, I32 = jnp.float32, jnp.bfloat16, jnp.int32
ROWS, WIDTH, HALF, HEAD_DIM = 512, 3072, 1536, 128
BLOCK = WIDTH + HALF + 128
KEY, VALUE, QUERY = 0, 1, 2
Q_TILE, SPANS, LOG2E = 256, (512, 640, 768, 896, 1024, 1280), 1.4426950408889634
PARTS = (
    (KEY, 0, 48, (1, 0, 2)),
    (KEY, 48, 48, (2, 0, 1)),
    (VALUE, 0, 48, (0, 1, 2)),
    (VALUE, 48, 48, (0, 2, 1)),
    (QUERY, 0, 48, (1, 2, 0)),
    (QUERY, 48, 32, (0, 1, 2)),
    (QUERY, 80, 16, (0, 2, 1)),
)
FRONT = 2432


def dot(a, b):
    return jnp.dot(a, b, preferred_element_type=F32)


def dot_nt(a, b):
    return lax.dot_general(a, b, (((1,), (1,)), ((), ())), preferred_element_type=F32)


def iota(shape, dim):
    return lax.broadcasted_iota(I32, shape, dim)


def one_hot(row_ids, lane_ids):
    return jnp.where(row_ids == lane_ids, 1.0, 0.0).astype(BF16)


def project_kernel(
    target, segment, bucket, mod_table, latents_in, w_query, w_key, w_value,
    q_out, k_out, v_out, seg_out, info_out,
    latents, q_made, k_made, v_made, outgoing, front, back, incoming, weights, hidden, tags, hits, keys, seg_all,
    z_send, z_recv, p_send, p_recv, w_send, w_recv, s_send, s_recv, x_send, x_recv, h_send, h_recv, f_send, f_recv, o_send, o_recv, o_local, local,
):
    me_dp, me_seq = lax.axis_index("dp"), lax.axis_index("seq")
    x_lo, z, y = me_dp // 16, (me_dp // 4) % 4, me_dp % 4
    x_hi, core = me_seq // 2, me_seq % 2
    me = (x_hi * 2 + x_lo, z, y)
    sibling = (me_dp, x_hi * 2 + (1 - core))

    def at_chip(c):
        return ((c[0] % 2) * 16 + c[1] * 4 + c[2], (c[0] // 2) * 2 + core)

    def along_z(dz):
        return (x_lo * 16 + ((z + dz) % 4) * 4 + y, me_seq)

    def in_plane(b, sign):
        return (((x_lo + b // 4) % 2) * 16 + z * 4 + (y + 4 + sign * (b % 4)) % 4, me_seq)

    def seq_peer(r):
        if r == 1:
            return sibling
        return (me_dp, (1 - x_hi) * 2 + (core if r == 2 else 1 - core))

    barrier = pltpu.get_barrier_semaphore()

    def greet(k, carry):
        pl.semaphore_signal(barrier, inc=1, device_id=((me_dp + k) % 32, me_seq), device_id_type=MESH)
        return carry

    lax.fori_loop(1, 32, greet, 0)
    for peer in (seq_peer(1), seq_peer(2), seq_peer(3), ((1 - x_lo) * 16 + z * 4 + y, (1 - x_hi) * 2 + core)):
        pl.semaphore_signal(barrier, inc=1, device_id=peer, device_id_type=MESH)

    load = pltpu.make_async_copy(latents_in, latents, local.at[3])
    load.start()
    own = []
    for m, shard in ((KEY, w_key), (VALUE, w_value), (QUERY, w_query)):
        copy = pltpu.make_async_copy(shard, weights.at[m, me[0], z, y], local.at[m])
        copy.start()
        own.append(copy)
    seg_all[me_seq] = jnp.broadcast_to(segment[...], (8, ROWS))
    pl.semaphore_wait(barrier, 35)

    shards = {KEY: w_key, VALUE: w_value, QUERY: w_query}

    def w_copy(p, phase, pos, off, sending=True):
        m, first_row, row_count, order = PARTS[p]
        axis, done = order[phase], order[:phase]
        index = [m]
        for ax in range(3):
            index.append(pos % 4 if ax == axis else slice(None) if ax in done else me[ax])
        index.append(pl.ds(first_row, row_count))
        there = list(me)
        there[axis] = (there[axis] + off) % 4
        piece = weights.at[tuple(index)]
        source = shards[m].at[pl.ds(first_row, row_count)] if phase == 0 and sending else piece
        return pltpu.make_async_remote_copy(
            src_ref=source, dst_ref=piece, send_sem=w_send.at[p, phase, off - 1], recv_sem=w_recv.at[p, phase, off - 1],
            device_id=at_chip(there), device_id_type=MESH,
        )

    def w_start(p, phase, offs=(1, 3, 2)):
        axis = PARTS[p][3][phase]
        for off in offs:
            w_copy(p, phase, me[axis], off).start()

    def w_arrived(p, phase):
        axis = PARTS[p][3][phase]
        for off in (1, 3, 2):
            w_copy(p, phase, me[axis] + 4 - off, off, False).wait_recv()

    for p in range(len(PARTS)):
        w_start(p, 0)

    def s_copy(r, slot):
        return pltpu.make_async_remote_copy(
            src_ref=seg_all.at[slot], dst_ref=seg_all.at[slot], send_sem=s_send.at[r - 1], recv_sem=s_recv.at[r - 1],
            device_id=seq_peer(r), device_id_type=MESH,
        )

    for r in (1, 2, 3):
        s_copy(r, me_seq).start()

    row = target[...] & (ROWS - 1)
    dest = target[...] >> 11
    block = ((((dest >> 2) & 3) + 4 - z) & 3) * 8 + (((dest >> 4) + x_lo) & 1) * 4 + (((dest & 3) + 4 - y) & 3)
    block_hit = jnp.where(iota((32, ROWS), 0) == block, 1.0, 0.0)
    before = one_hot(jnp.minimum(iota((ROWS, ROWS), 0) + 1, iota((ROWS, ROWS), 1)), iota((ROWS, ROWS), 0) + 1)
    earlier = dot(block_hit.astype(BF16), before)
    rank = jnp.sum(block_hit * earlier, axis=0, keepdims=True).astype(I32)
    late = rank >= 16
    keys[0:1] = jnp.where(late, -1, block * 16 + rank)
    keys[1:2] = jnp.where(late, block * 16 + rank - 16, -1)
    keys[2:3] = jnp.where(late, block * 16 + rank - 8, -1)
    token_bucket = jnp.zeros((1, ROWS), I32)
    for clip in range(8):
        token_bucket += jnp.where(segment[...] == clip, bucket[:, clip : clip + 1], 0)
    stacked = jnp.concatenate([row.astype(F32), token_bucket.astype(F32), jnp.zeros((6, ROWS), F32)], axis=0)
    columns = jnp.transpose(stacked)
    row_col, bucket_col = columns[:, 0:1], columns[:, 1:2]
    lane = iota((ROWS, 128), 1)
    hits[...] = jnp.where(bucket_col == lane.astype(F32), 1.0, 0.0).astype(BF16)
    high = jnp.where(row_col >= 256.0, 1.0, 0.0)
    low = row_col - 256.0 * high
    kind = lane % 3
    tag = jnp.where(kind == 0, low, jnp.where(kind == 1, high, 1.0))
    tags[0] = jnp.where(lane < 3, tag, 0.0).astype(BF16)
    tags[1] = jnp.where((lane >= 3) & (lane < 6), tag, 0.0).astype(BF16)

    fore, aft = pl.ds(0, FRONT), pl.ds(FRONT, BLOCK - FRONT)

    def z_copy(stage, dz, sign):
        if stage == 0:
            src, dst = outgoing.at[dz, :, :, fore], front.at[dz]
        else:
            src, dst = back.at[dz], incoming.at[dz, :, :, aft]
        return pltpu.make_async_remote_copy(
            src_ref=src, dst_ref=dst, send_sem=z_send.at[stage, dz], recv_sem=z_recv.at[stage, dz],
            device_id=along_z(dz if sign > 0 else 4 - dz), device_id_type=MESH,
        )

    def p_copy(stage, b, sign):
        if stage == 0:
            src, dst = outgoing.at[:, b, :, aft], back.at[:, b]
        else:
            src, dst = front.at[:, b], incoming.at[:, b, :, fore]
        return pltpu.make_async_remote_copy(
            src_ref=src, dst_ref=dst, send_sem=p_send.at[stage, b], recv_sem=p_recv.at[stage, b],
            device_id=in_plane(b, sign), device_id_type=MESH,
        )

    z_order, p_order = (1, 3, 2), (1, 4, 3, 5, 2, 7, 6)

    def stay(src, dst, i):
        copy = pltpu.make_async_copy(src, dst, local.at[i])
        copy.start()
        return copy

    def pack(c, carry):
        dz = (c + 1) % 4
        base = dz * 128
        ids = iota((128, ROWS), 0) + base
        first = one_hot(ids, keys[0:1])
        left = one_hot(ids, keys[1:2])
        right = one_hot(ids, keys[2:3])

        def put(lo, hi, value):
            outgoing[dz, :, :, lo:hi] = value.astype(BF16).reshape(8, 16, hi - lo)

        put(0, WIDTH, dot(first, latents[...]))
        put(WIDTH, WIDTH + HALF, dot(left, latents[:, 0:HALF]) + dot(right, latents[:, HALF:WIDTH]))
        put(WIDTH + HALF, BLOCK, dot(first, tags[0]) + dot(left + right, tags[1]))

        @pl.when(c < 3)
        def _():
            z_copy(0, dz, 1).start()

        return carry

    for copy in own:
        copy.wait()
    for p in range(len(PARTS)):
        w_arrived(p, 0)
        w_start(p, 1)
    load.wait()
    lax.fori_loop(0, 4, pack, 0)

    for b in p_order:
        p_copy(0, b, 1).start()
    stays = [stay(outgoing.at[0, :, :, fore], front.at[0], 0), stay(outgoing.at[:, 0, :, aft], back.at[:, 0], 1)]
    for r in (1, 2, 3):
        s_copy(r, (seq_peer(r)[1])).wait_recv()
    for i in range(3):
        seg_out[:, 512 * i : 512 * i + 512] = seg_all[x_hi + i]

    window = seg_out[0:1, :]
    info_lane = iota((1, 128), 1)
    for t in range(ROWS // Q_TILE):
        base = pl.multiple_of((x_hi + core) * ROWS + t * Q_TILE, 128)
        ids = seg_out[0:1, pl.ds(base, Q_TILE)]
        first = jnp.sum(jnp.where(window < ids[:, 0:1], 1, 0), axis=1, keepdims=True)
        last = jnp.sum(jnp.where(window <= ids[:, Q_TILE - 1 :], 1, 0), axis=1, keepdims=True)
        info_out[t : t + 1, :] = jnp.where(info_lane == 0, first, jnp.where(info_lane == 1, last, base))

    for copy in stays:
        copy.wait()
    for dz in z_order:
        z_copy(0, dz, -1).wait_recv()
    for b in p_order:
        p_copy(1, b, 1).start()
    for b in p_order:
        p_copy(0, b, -1).wait_recv()
    for dz in z_order:
        z_copy(1, dz, 1).start()
    stays = [stay(front.at[:, 0], incoming.at[:, 0, :, fore], 0), stay(back.at[0], incoming.at[0, :, :, aft], 1)]
    for p in (0, 1):
        w_arrived(p, 1)
        w_start(p, 2, (2,))
    for p in range(2, len(PARTS)):
        w_arrived(p, 1)
    for copy in stays:
        copy.wait()
    for dz in z_order:
        z_copy(1, dz, -1).wait_recv()
    for b in p_order:
        p_copy(1, b, -1).wait_recv()
    for p in (0, 1):
        w_start(p, 2, (1, 3))
        w_start(p + 2, 2, (2,))
    w_start(4, 2)

    def received(lo, hi):
        return incoming[:, :, :, lo:hi].reshape(ROWS, hi - lo)

    own_slot, sib_slot, halo_slot = x_hi + core, x_hi + 1 - core, 2 - 2 * x_hi
    pick_lane = iota((8, 128), 1)
    pick_row = iota((8, 128), 0)
    pick_kind = pick_lane - 3 * pick_row
    pick = jnp.where(
        pick_row < 2,
        jnp.where(pick_kind == 0, 1.0, jnp.where(pick_kind == 1, 256.0, jnp.where(pick_kind == 2, 512.0, 0.0))),
        0.0,
    ).astype(BF16)
    rows_in = dot_nt(pick, received(WIDTH + HALF, BLOCK)).astype(I32) - 512
    odd = (iota((1, ROWS), 1) & 15) >= 8
    keys[0:1] = rows_in[0:1]
    keys[1:2] = jnp.where(odd, -1, rows_in[1:2])
    keys[2:3] = jnp.where(odd, rows_in[1:2], -1)

    def chunk(slot, c):
        return hidden.at[slot, pl.ds(pl.multiple_of(c * 128, 128), 128)]

    def x_copy(slot, c):
        return pltpu.make_async_remote_copy(
            src_ref=chunk(slot, c), dst_ref=chunk(slot, c), send_sem=x_send.at[c], recv_sem=x_recv.at[c],
            device_id=sibling, device_id_type=MESH,
        )

    def h_copy(c):
        return pltpu.make_async_remote_copy(
            src_ref=chunk(own_slot, c), dst_ref=chunk(2 * x_hi, c), send_sem=h_send.at[c], recv_sem=h_recv.at[c % 2],
            device_id=(me_dp, (1 - x_hi) * 2 + c // 2), device_id_type=MESH,
        )

    def f_copy(i, owner):
        c = 2 * owner + i
        return pltpu.make_async_remote_copy(
            src_ref=chunk(halo_slot, c), dst_ref=chunk(halo_slot, c), send_sem=f_send.at[i], recv_sem=f_recv.at[i],
            device_id=sibling, device_id_type=MESH,
        )

    on_edge = x_hi + core == 1

    def place(c, carry):
        base = pl.multiple_of(c * 128, 128)
        rows = pl.ds(base, 128)
        ids = iota((128, ROWS), 0) + base
        whole = dot(one_hot(ids, keys[0:1]), received(0, WIDTH))
        left = dot(one_hot(ids, keys[1:2]), received(WIDTH, WIDTH + HALF))
        right = dot(one_hot(ids, keys[2:3]), received(WIDTH, WIDTH + HALF))
        placed = whole + jnp.concatenate([left, right], axis=1)
        centered = placed - jnp.mean(placed, axis=1, keepdims=True)
        var = jnp.mean(centered * centered, axis=1, keepdims=True)
        normalized = centered * lax.rsqrt(var + 1e-6)
        modulation = dot(hits[rows, 0:16], mod_table[...])
        hidden[own_slot, rows] = (normalized * (1.0 + modulation[:, WIDTH:]) + modulation[:, :WIDTH]).astype(BF16)
        x_copy(own_slot, c).start()

        @pl.when(on_edge)
        def _():
            h_copy(c).start()

        return carry

    lax.fori_loop(0, 4, place, 0)

    made, outs = (k_made, v_made, q_made), (k_out, v_out, q_out)

    def project(m, slot, at):
        def step(r, carry):
            w = jnp.concatenate([weights[m, 2 * h : 2 * h + 2].reshape(WIDTH, 384) for h in range(2)], axis=1)
            rows = pl.ds(pl.multiple_of(r * 256, 256), 256)
            result = dot(hidden[slot, rows], w).astype(BF16)
            for h in range(2):
                made[m][h, pl.ds(pl.multiple_of(at * ROWS + r * 256, 256), 256)] = result[:, 384 * h : 384 * h + 384]
            return carry

        lax.fori_loop(0, 2, step, 0)

    def o_there(m, at, to, owner):
        return pltpu.make_async_remote_copy(
            src_ref=made[m].at[:, pl.ds(pl.multiple_of(at * ROWS, ROWS), ROWS)],
            dst_ref=outs[m].at[owner, :, pl.ds(pl.multiple_of(to * ROWS, ROWS), ROWS)],
            send_sem=o_send.at[m, to], recv_sem=o_recv.at[m, to], device_id=sibling, device_id_type=MESH,
        )

    def o_here(m, at, to):
        return pltpu.make_async_copy(
            made[m].at[:, pl.ds(pl.multiple_of(at * ROWS, ROWS), ROWS)],
            outs[m].at[core, :, pl.ds(pl.multiple_of(to * ROWS, ROWS), ROWS)],
            o_local.at[m, to],
        )

    def make(m, slot):
        project(m, slot, slot)
        o_there(m, slot, slot, core).start()
        o_here(m, slot, slot).start()

    for p in (0, 1):
        w_arrived(p, 2)
        w_start(p + 2, 2, (1, 3))
    for p in (5, 6):
        w_start(p, 2, (2,))
    make(KEY, own_slot)
    for c in range(4):
        x_copy(sib_slot, c).wait_recv()
    make(KEY, sib_slot)
    for p in (2, 3):
        w_arrived(p, 2)
    for p in (5, 6):
        w_start(p, 2, (1, 3))
    make(VALUE, own_slot)
    make(VALUE, sib_slot)
    for i in range(2):
        h_copy(2 * core + i).wait_recv()
        f_copy(i, core).start()
    for i in range(2):
        f_copy(i, 1 - core).wait_recv()
    make(KEY, halo_slot)
    make(VALUE, halo_slot)
    for p in (4, 5, 6):
        w_arrived(p, 2)
    project(QUERY, sib_slot, 1)
    o_there(QUERY, 1, 0, core).start()
    project(QUERY, own_slot, 0)
    o_here(QUERY, 0, 0).start()

    for m in (KEY, VALUE):
        for slot in range(3):
            o_here(m, slot, slot).wait()
            o_there(m, slot, slot, core).wait_send()
            o_there(m, slot, slot, 1 - core).wait_recv()
    o_here(QUERY, 0, 0).wait()
    o_there(QUERY, 1, 0, core).wait_send()
    o_there(QUERY, 1, 0, 1 - core).wait_recv()

    for r in (1, 2, 3):
        s_copy(r, me_seq).wait_send()
    for stage in (0, 1):
        for dz in z_order:
            z_copy(stage, dz, 1).wait_send()
        for b in p_order:
            p_copy(stage, b, 1).wait_send()
    for p in range(len(PARTS)):
        for phase in range(3):
            for off in (1, 3, 2):
                w_copy(p, phase, me[PARTS[p][3][phase]], off).wait_send()
    for c in range(4):
        x_copy(own_slot, c).wait_send()

    @pl.when(on_edge)
    def _():
        for c in range(4):
            h_copy(c).wait_send()

    for i in range(2):
        f_copy(i, core).wait_send()


def project_tokens(target, segment, bucket, mod_table, latents_in, w_query, w_key, w_value):
    vmem = pl.BlockSpec(memory_space=pltpu.VMEM)
    anywhere = pl.BlockSpec(memory_space=pl.ANY)
    dma = pltpu.SemaphoreType.DMA
    return pl.pallas_call(
        project_kernel,
        out_shape=(
            jax.ShapeDtypeStruct((2, 2, ROWS, 384), BF16),
            jax.ShapeDtypeStruct((2, 2, 3 * ROWS, 384), BF16),
            jax.ShapeDtypeStruct((2, 2, 3 * ROWS, 384), BF16),
            jax.ShapeDtypeStruct((8, 3 * ROWS), I32),
            jax.ShapeDtypeStruct((ROWS // Q_TILE, 128), I32),
        ),
        in_specs=[vmem] * 4 + [anywhere] * 4,
        out_specs=(anywhere,) * 3 + (vmem,) * 2,
        scratch_shapes=[
            pltpu.VMEM((ROWS, WIDTH), BF16),
            pltpu.VMEM((2, 2 * ROWS, 384), BF16),
            pltpu.VMEM((2, 3 * ROWS, 384), BF16),
            pltpu.VMEM((2, 3 * ROWS, 384), BF16),
            pltpu.VMEM((4, 8, 16, BLOCK), BF16),
            pltpu.VMEM((4, 8, 16, FRONT), BF16),
            pltpu.VMEM((4, 8, 16, BLOCK - FRONT), BF16),
            pltpu.VMEM((4, 8, 16, BLOCK), BF16),
            pltpu.VMEM((3, 4, 4, 4, 96, 384), BF16),
            pltpu.VMEM((3, ROWS, WIDTH), BF16),
            pltpu.VMEM((2, ROWS, 128), BF16),
            pltpu.VMEM((ROWS, 128), BF16),
            pltpu.VMEM((8, ROWS), I32),
            pltpu.VMEM((4, 8, ROWS), I32),
            dma((2, 4)), dma((2, 4)), dma((2, 8)), dma((2, 8)), dma((len(PARTS), 3, 3)), dma((len(PARTS), 3, 3)), dma((3,)), dma((3,)),
            dma((4,)), dma((4,)), dma((4,)), dma((2,)), dma((2,)), dma((2,)), dma((3, 3)), dma((3, 3)), dma((3, 3)), dma((4,)),
        ],
        compiler_params=pltpu.CompilerParams(collective_id=0, has_side_effects=True, vmem_limit_bytes=60 * 2**20),
        name="project_tokens",
    )(target, segment, bucket, mod_table, latents_in, w_query, w_key, w_value)


def attend_kernel(info, q, k, v, seg, out):
    tile = pl.program_id(1)
    begin = (info[tile, 0] // 128) * 128
    span = info[tile, 1] - begin
    base = pl.multiple_of(info[tile, 2], 128)
    seg_query = jnp.transpose(seg[:, pl.ds(base, Q_TILE)].astype(F32))[:, 0:1]

    def over(width):
        start = pl.multiple_of(jnp.minimum(begin, 3 * ROWS - width), 128)
        rows = pl.ds(start, width)
        bias = jnp.where(seg_query == seg[0:1, rows].astype(F32), 0.0, -1e30)
        ones = jnp.ones((width, HEAD_DIM), BF16)
        heads = [(g, slice(e * HEAD_DIM, (e + 1) * HEAD_DIM)) for g in range(2) for e in range(3)]

        def score(g, cols):
            return dot_nt(q[g, 0, :, cols], k[g, 0, rows, cols]) + bias

        ready = score(*heads[0])
        for i, (g, cols) in enumerate(heads):
            scores = ready
            if i + 1 < len(heads):
                ready = score(*heads[i + 1])
            weight = jnp.exp2((scores - jnp.max(scores, axis=1, keepdims=True)) * (HEAD_DIM**-0.5 * LOG2E))
            mixed = dot(weight.astype(BF16), jnp.concatenate([v[g, 0, rows, cols], ones], axis=1))
            out[:, g * 384 + cols.start : g * 384 + cols.stop] = (mixed[:, :HEAD_DIM] / mixed[:, HEAD_DIM:]).astype(BF16)

    least = -1
    for width in SPANS:
        pl.when((span > least) & (span <= width))(functools.partial(over, width))
        least = width


def attend(info, q, k, v, seg):
    return pl.pallas_call(
        attend_kernel,
        out_shape=jax.ShapeDtypeStruct((ROWS, 1536), BF16),
        grid_spec=pltpu.PrefetchScalarGridSpec(
            num_scalar_prefetch=1,
            grid=(2, ROWS // Q_TILE),
            in_specs=[
                pl.BlockSpec((2, 1, Q_TILE, 384), lambda h, t, info: (0, h, t, 0)),
                pl.BlockSpec((2, 1, 3 * ROWS, 384), lambda h, t, info: (0, h, 0, 0)),
                pl.BlockSpec((2, 1, 3 * ROWS, 384), lambda h, t, info: (0, h, 0, 0)),
                pl.BlockSpec((8, 3 * ROWS), lambda h, t, info: (0, 0)),
            ],
            out_specs=pl.BlockSpec((Q_TILE, 768), lambda h, t, info: (t, h)),
        ),
        compiler_params=pltpu.CompilerParams(vmem_limit_bytes=60 * 2**20),
        name="attend",
    )(info, q, k, v, seg)


def on_device(latents, target, segment_ids, clip_bucket, mod_table, w_query, w_key, w_value):
    q, k, v, seg, info = project_tokens(
        target.reshape(1, ROWS), segment_ids, clip_bucket, mod_table, latents, w_query, w_key, w_value
    )
    return attend(info, q, k, v, seg)


def solution(mesh):
    in_specs = (
        P(("dp", "seq"), None),
        P(("dp", "seq")),
        P("dp", "seq"),
        P("dp", None),
        P(),
        P("dp", "seq"),
        P("dp", "seq"),
        P("dp", "seq"),
    )
    out_specs = P(("dp", "seq"), None)
    return jax.shard_map(on_device, mesh=mesh, in_specs=in_specs, out_specs=out_specs, check_vma=False)
```

```python
import functools

import jax
import jax.numpy as jnp
from jax import lax
from jax.experimental import pallas as pl
from jax.experimental.pallas import tpu as pltpu
from jax.sharding import PartitionSpec as P

MESH = pl.DeviceIdType.MESH
F32, BF16, I32 = jnp.float32, jnp.bfloat16, jnp.int32
ROWS, WIDTH, HALF, HEAD_DIM = 512, 3072, 1536, 128
BLOCK = WIDTH + HALF + 128
KEY, VALUE, QUERY = 0, 1, 2
Q_TILE, SPANS, LOG2E = 256, (512, 640, 768, 896, 1024, 1280), 1.4426950408889634
PARTS = (
    (KEY, 0, 48, (1, 0, 2)),
    (KEY, 48, 48, (2, 0, 1)),
    (VALUE, 0, 48, (0, 1, 2)),
    (VALUE, 48, 48, (0, 2, 1)),
    (QUERY, 0, 48, (1, 2, 0)),
    (QUERY, 48, 32, (0, 1, 2)),
    (QUERY, 80, 16, (0, 2, 1)),
)
FRONT = 2432


def dot(a, b):
    return jnp.dot(a, b, preferred_element_type=F32)


def dot_nt(a, b):
    return lax.dot_general(a, b, (((1,), (1,)), ((), ())), preferred_element_type=F32)


def iota(shape, dim):
    return lax.broadcasted_iota(I32, shape, dim)


def one_hot(row_ids, lane_ids):
    return jnp.where(row_ids == lane_ids, 1.0, 0.0).astype(BF16)


def project_kernel(
    target, segment, bucket, mod_table, latents_in, w_query, w_key, w_value,
    q_out, k_out, v_out, seg_out, info_out,
    latents, q_made, k_made, v_made, outgoing, front, back, incoming, weights, hidden, tags, hits, keys, seg_all,
    z_send, z_recv, p_send, p_recv, w_send, w_recv, s_send, s_recv, x_send, x_recv, h_send, h_recv, f_send, f_recv, o_send, o_recv, o_local, local,
):
    me_dp, me_seq = lax.axis_index("dp"), lax.axis_index("seq")
    x_lo, z, y = me_dp // 16, (me_dp // 4) % 4, me_dp % 4
    x_hi, core = me_seq // 2, me_seq % 2
    me = (x_hi * 2 + x_lo, z, y)
    sibling = (me_dp, x_hi * 2 + (1 - core))

    def at_chip(c):
        return ((c[0] % 2) * 16 + c[1] * 4 + c[2], (c[0] // 2) * 2 + core)

    def along_z(dz):
        return (x_lo * 16 + ((z + dz) % 4) * 4 + y, me_seq)

    def in_plane(b, sign):
        return (((x_lo + b // 4) % 2) * 16 + z * 4 + (y + 4 + sign * (b % 4)) % 4, me_seq)

    def seq_peer(r):
        if r == 1:
            return sibling
        return (me_dp, (1 - x_hi) * 2 + (core if r == 2 else 1 - core))

    barrier = pltpu.get_barrier_semaphore()

    def greet(k, carry):
        pl.semaphore_signal(barrier, inc=1, device_id=((me_dp + k) % 32, me_seq), device_id_type=MESH)
        return carry

    lax.fori_loop(1, 32, greet, 0)
    for peer in (seq_peer(1), seq_peer(2), seq_peer(3), ((1 - x_lo) * 16 + z * 4 + y, (1 - x_hi) * 2 + core)):
        pl.semaphore_signal(barrier, inc=1, device_id=peer, device_id_type=MESH)

    load = pltpu.make_async_copy(latents_in, latents, local.at[3])
    load.start()
    own = []
    for m, shard in ((KEY, w_key), (VALUE, w_value), (QUERY, w_query)):
        copy = pltpu.make_async_copy(shard, weights.at[m, me[0], z, y], local.at[m])
        copy.start()
        own.append(copy)
    seg_all[me_seq] = jnp.broadcast_to(segment[...], (8, ROWS))
    pl.semaphore_wait(barrier, 35)

    shards = {KEY: w_key, VALUE: w_value, QUERY: w_query}

    def w_copy(p, phase, pos, off, sending=True):
        m, first_row, row_count, order = PARTS[p]
        axis, done = order[phase], order[:phase]
        index = [m]
        for ax in range(3):
            index.append(pos % 4 if ax == axis else slice(None) if ax in done else me[ax])
        index.append(pl.ds(first_row, row_count))
        there = list(me)
        there[axis] = (there[axis] + off) % 4
        piece = weights.at[tuple(index)]
        source = shards[m].at[pl.ds(first_row, row_count)] if phase == 0 and sending else piece
        return pltpu.make_async_remote_copy(
            src_ref=source, dst_ref=piece, send_sem=w_send.at[p, phase, off - 1], recv_sem=w_recv.at[p, phase, off - 1],
            device_id=at_chip(there), device_id_type=MESH,
        )

    def w_start(p, phase, offs=(1, 3, 2)):
        axis = PARTS[p][3][phase]
        for off in offs:
            w_copy(p, phase, me[axis], off).start()

    def w_arrived(p, phase):
        axis = PARTS[p][3][phase]
        for off in (1, 3, 2):
            w_copy(p, phase, me[axis] + 4 - off, off, False).wait_recv()

    for p in range(len(PARTS)):
        w_start(p, 0)

    def s_copy(r, slot):
        return pltpu.make_async_remote_copy(
            src_ref=seg_all.at[slot], dst_ref=seg_all.at[slot], send_sem=s_send.at[r - 1], recv_sem=s_recv.at[r - 1],
            device_id=seq_peer(r), device_id_type=MESH,
        )

    for r in (1, 2, 3):
        s_copy(r, me_seq).start()

    row = target[...] & (ROWS - 1)
    dest = target[...] >> 11
    block = ((((dest >> 2) & 3) + 4 - z) & 3) * 8 + (((dest >> 4) + x_lo) & 1) * 4 + (((dest & 3) + 4 - y) & 3)
    block_hit = jnp.where(iota((32, ROWS), 0) == block, 1.0, 0.0)
    before = one_hot(jnp.minimum(iota((ROWS, ROWS), 0) + 1, iota((ROWS, ROWS), 1)), iota((ROWS, ROWS), 0) + 1)
    earlier = dot(block_hit.astype(BF16), before)
    rank = jnp.sum(block_hit * earlier, axis=0, keepdims=True).astype(I32)
    late = rank >= 16
    keys[0:1] = jnp.where(late, -1, block * 16 + rank)
    keys[1:2] = jnp.where(late, block * 16 + rank - 16, -1)
    keys[2:3] = jnp.where(late, block * 16 + rank - 8, -1)
    token_bucket = jnp.zeros((1, ROWS), I32)
    for clip in range(8):
        token_bucket += jnp.where(segment[...] == clip, bucket[:, clip : clip + 1], 0)
    stacked = jnp.concatenate([row.astype(F32), token_bucket.astype(F32), jnp.zeros((6, ROWS), F32)], axis=0)
    columns = jnp.transpose(stacked)
    row_col, bucket_col = columns[:, 0:1], columns[:, 1:2]
    lane = iota((ROWS, 128), 1)
    hits[...] = jnp.where(bucket_col == lane.astype(F32), 1.0, 0.0).astype(BF16)
    high = jnp.where(row_col >= 256.0, 1.0, 0.0)
    low = row_col - 256.0 * high
    kind = lane % 3
    tag = jnp.where(kind == 0, low, jnp.where(kind == 1, high, 1.0))
    tags[0] = jnp.where(lane < 3, tag, 0.0).astype(BF16)
    tags[1] = jnp.where((lane >= 3) & (lane < 6), tag, 0.0).astype(BF16)

    fore, aft = pl.ds(0, FRONT), pl.ds(FRONT, BLOCK - FRONT)

    def z_copy(stage, dz, sign):
        if stage == 0:
            src, dst = outgoing.at[dz, :, :, fore], front.at[dz]
        else:
            src, dst = back.at[dz], incoming.at[dz, :, :, aft]
        return pltpu.make_async_remote_copy(
            src_ref=src, dst_ref=dst, send_sem=z_send.at[stage, dz], recv_sem=z_recv.at[stage, dz],
            device_id=along_z(dz if sign > 0 else 4 - dz), device_id_type=MESH,
        )

    def p_copy(stage, b, sign):
        if stage == 0:
            src, dst = outgoing.at[:, b, :, aft], back.at[:, b]
        else:
            src, dst = front.at[:, b], incoming.at[:, b, :, fore]
        return pltpu.make_async_remote_copy(
            src_ref=src, dst_ref=dst, send_sem=p_send.at[stage, b], recv_sem=p_recv.at[stage, b],
            device_id=in_plane(b, sign), device_id_type=MESH,
        )

    z_order, p_order = (1, 3, 2), (1, 4, 3, 5, 2, 7, 6)

    def stay(src, dst, i):
        copy = pltpu.make_async_copy(src, dst, local.at[i])
        copy.start()
        return copy

    def pack(c, carry):
        dz = (c + 1) % 4
        base = dz * 128
        ids = iota((128, ROWS), 0) + base
        first = one_hot(ids, keys[0:1])
        left = one_hot(ids, keys[1:2])
        right = one_hot(ids, keys[2:3])

        def put(lo, hi, value):
            outgoing[dz, :, :, lo:hi] = value.astype(BF16).reshape(8, 16, hi - lo)

        put(0, WIDTH, dot(first, latents[...]))
        put(WIDTH, WIDTH + HALF, dot(left, latents[:, 0:HALF]) + dot(right, latents[:, HALF:WIDTH]))
        put(WIDTH + HALF, BLOCK, dot(first, tags[0]) + dot(left + right, tags[1]))

        @pl.when(c < 3)
        def _():
            z_copy(0, dz, 1).start()

        return carry

    for copy in own:
        copy.wait()
    for p in range(len(PARTS)):
        w_arrived(p, 0)
        w_start(p, 1)
    load.wait()
    lax.fori_loop(0, 4, pack, 0)

    for b in p_order:
        p_copy(0, b, 1).start()
    stays = [stay(outgoing.at[0, :, :, fore], front.at[0], 0), stay(outgoing.at[:, 0, :, aft], back.at[:, 0], 1)]
    for r in (1, 2, 3):
        s_copy(r, (seq_peer(r)[1])).wait_recv()
    for i in range(3):
        seg_out[:, 512 * i : 512 * i + 512] = seg_all[x_hi + i]

    window = seg_out[0:1, :]
    info_lane = iota((1, 128), 1)
    for t in range(ROWS // Q_TILE):
        base = pl.multiple_of((x_hi + core) * ROWS + t * Q_TILE, 128)
        ids = seg_out[0:1, pl.ds(base, Q_TILE)]
        first = jnp.sum(jnp.where(window < ids[:, 0:1], 1, 0), axis=1, keepdims=True)
        last = jnp.sum(jnp.where(window <= ids[:, Q_TILE - 1 :], 1, 0), axis=1, keepdims=True)
        info_out[t : t + 1, :] = jnp.where(info_lane == 0, first, jnp.where(info_lane == 1, last, base))

    for copy in stays:
        copy.wait()
    for dz in z_order:
        z_copy(0, dz, -1).wait_recv()
    for b in p_order:
        p_copy(1, b, 1).start()
    for b in p_order:
        p_copy(0, b, -1).wait_recv()
    for dz in z_order:
        z_copy(1, dz, 1).start()
    stays = [stay(front.at[:, 0], incoming.at[:, 0, :, fore], 0), stay(back.at[0], incoming.at[0, :, :, aft], 1)]
    for p in (0, 1):
        w_arrived(p, 1)
        w_start(p, 2, (2,))
    for p in range(2, len(PARTS)):
        w_arrived(p, 1)
    for copy in stays:
        copy.wait()
    for dz in z_order:
        z_copy(1, dz, -1).wait_recv()
    for b in p_order:
        p_copy(1, b, -1).wait_recv()
    for p in (0, 1):
        w_start(p, 2, (1, 3))
        w_start(p + 2, 2, (2,))
    w_start(4, 2)

    def received(lo, hi):
        return incoming[:, :, :, lo:hi].reshape(ROWS, hi - lo)

    own_slot, sib_slot, halo_slot = x_hi + core, x_hi + 1 - core, 2 - 2 * x_hi
    pick_lane = iota((8, 128), 1)
    pick_row = iota((8, 128), 0)
    pick_kind = pick_lane - 3 * pick_row
    pick = jnp.where(
        pick_row < 2,
        jnp.where(pick_kind == 0, 1.0, jnp.where(pick_kind == 1, 256.0, jnp.where(pick_kind == 2, 512.0, 0.0))),
        0.0,
    ).astype(BF16)
    rows_in = dot_nt(pick, received(WIDTH + HALF, BLOCK)).astype(I32) - 512
    odd = (iota((1, ROWS), 1) & 15) >= 8
    keys[0:1] = rows_in[0:1]
    keys[1:2] = jnp.where(odd, -1, rows_in[1:2])
    keys[2:3] = jnp.where(odd, rows_in[1:2], -1)

    def chunk(slot, c):
        return hidden.at[slot, pl.ds(pl.multiple_of(c * 128, 128), 128)]

    def x_copy(slot, c):
        return pltpu.make_async_remote_copy(
            src_ref=chunk(slot, c), dst_ref=chunk(slot, c), send_sem=x_send.at[c], recv_sem=x_recv.at[c],
            device_id=sibling, device_id_type=MESH,
        )

    def h_copy(c):
        return pltpu.make_async_remote_copy(
            src_ref=chunk(own_slot, c), dst_ref=chunk(2 * x_hi, c), send_sem=h_send.at[c], recv_sem=h_recv.at[c % 2],
            device_id=(me_dp, (1 - x_hi) * 2 + c // 2), device_id_type=MESH,
        )

    def f_copy(i, owner):
        c = 2 * owner + i
        return pltpu.make_async_remote_copy(
            src_ref=chunk(halo_slot, c), dst_ref=chunk(halo_slot, c), send_sem=f_send.at[i], recv_sem=f_recv.at[i],
            device_id=sibling, device_id_type=MESH,
        )

    on_edge = x_hi + core == 1

    def place(c, carry):
        base = pl.multiple_of(c * 128, 128)
        rows = pl.ds(base, 128)
        ids = iota((128, ROWS), 0) + base
        whole = dot(one_hot(ids, keys[0:1]), received(0, WIDTH))
        left = dot(one_hot(ids, keys[1:2]), received(WIDTH, WIDTH + HALF))
        right = dot(one_hot(ids, keys[2:3]), received(WIDTH, WIDTH + HALF))
        placed = whole + jnp.concatenate([left, right], axis=1)
        centered = placed - jnp.mean(placed, axis=1, keepdims=True)
        var = jnp.mean(centered * centered, axis=1, keepdims=True)
        normalized = centered * lax.rsqrt(var + 1e-6)
        modulation = dot(hits[rows, 0:16], mod_table[...])
        hidden[own_slot, rows] = (normalized * (1.0 + modulation[:, WIDTH:]) + modulation[:, :WIDTH]).astype(BF16)
        x_copy(own_slot, c).start()

        @pl.when(on_edge)
        def _():
            h_copy(c).start()

        return carry

    lax.fori_loop(0, 4, place, 0)

    made, outs = (k_made, v_made, q_made), (k_out, v_out, q_out)

    def project(m, slot, at):
        def step(r, carry):
            w = jnp.concatenate([weights[m, 2 * h : 2 * h + 2].reshape(WIDTH, 384) for h in range(2)], axis=1)
            rows = pl.ds(pl.multiple_of(r * 256, 256), 256)
            result = dot(hidden[slot, rows], w).astype(BF16)
            for h in range(2):
                made[m][h, pl.ds(pl.multiple_of(at * ROWS + r * 256, 256), 256)] = result[:, 384 * h : 384 * h + 384]
            return carry

        lax.fori_loop(0, 2, step, 0)

    def o_there(m, at, to, owner):
        return pltpu.make_async_remote_copy(
            src_ref=made[m].at[:, pl.ds(pl.multiple_of(at * ROWS, ROWS), ROWS)],
            dst_ref=outs[m].at[owner, :, pl.ds(pl.multiple_of(to * ROWS, ROWS), ROWS)],
            send_sem=o_send.at[m, to], recv_sem=o_recv.at[m, to], device_id=sibling, device_id_type=MESH,
        )

    def o_here(m, at, to):
        return pltpu.make_async_copy(
            made[m].at[:, pl.ds(pl.multiple_of(at * ROWS, ROWS), ROWS)],
            outs[m].at[core, :, pl.ds(pl.multiple_of(to * ROWS, ROWS), ROWS)],
            o_local.at[m, to],
        )

    def make(m, slot):
        project(m, slot, slot)
        o_there(m, slot, slot, core).start()
        o_here(m, slot, slot).start()

    for p in (0, 1):
        w_arrived(p, 2)
        w_start(p + 2, 2, (1, 3))
    for p in (5, 6):
        w_start(p, 2)
    make(KEY, own_slot)
    for c in range(4):
        x_copy(sib_slot, c).wait_recv()
    make(KEY, sib_slot)
    for p in (2, 3):
        w_arrived(p, 2)
    make(VALUE, own_slot)
    make(VALUE, sib_slot)
    for i in range(2):
        h_copy(2 * core + i).wait_recv()
        f_copy(i, core).start()
    for i in range(2):
        f_copy(i, 1 - core).wait_recv()
    make(KEY, halo_slot)
    make(VALUE, halo_slot)
    for p in (4, 5, 6):
        w_arrived(p, 2)
    project(QUERY, sib_slot, 1)
    o_there(QUERY, 1, 0, core).start()
    project(QUERY, own_slot, 0)
    o_here(QUERY, 0, 0).start()

    for m in (KEY, VALUE):
        for slot in range(3):
            o_here(m, slot, slot).wait()
            o_there(m, slot, slot, core).wait_send()
            o_there(m, slot, slot, 1 - core).wait_recv()
    o_here(QUERY, 0, 0).wait()
    o_there(QUERY, 1, 0, core).wait_send()
    o_there(QUERY, 1, 0, 1 - core).wait_recv()

    for r in (1, 2, 3):
        s_copy(r, me_seq).wait_send()
    for stage in (0, 1):
        for dz in z_order:
            z_copy(stage, dz, 1).wait_send()
        for b in p_order:
            p_copy(stage, b, 1).wait_send()
    for p in range(len(PARTS)):
        for phase in range(3):
            for off in (1, 3, 2):
                w_copy(p, phase, me[PARTS[p][3][phase]], off).wait_send()
    for c in range(4):
        x_copy(own_slot, c).wait_send()

    @pl.when(on_edge)
    def _():
        for c in range(4):
            h_copy(c).wait_send()

    for i in range(2):
        f_copy(i, core).wait_send()


def project_tokens(target, segment, bucket, mod_table, latents_in, w_query, w_key, w_value):
    vmem = pl.BlockSpec(memory_space=pltpu.VMEM)
    anywhere = pl.BlockSpec(memory_space=pl.ANY)
    dma = pltpu.SemaphoreType.DMA
    return pl.pallas_call(
        project_kernel,
        out_shape=(
            jax.ShapeDtypeStruct((2, 2, ROWS, 384), BF16),
            jax.ShapeDtypeStruct((2, 2, 3 * ROWS, 384), BF16),
            jax.ShapeDtypeStruct((2, 2, 3 * ROWS, 384), BF16),
            jax.ShapeDtypeStruct((8, 3 * ROWS), I32),
            jax.ShapeDtypeStruct((ROWS // Q_TILE, 128), I32),
        ),
        in_specs=[vmem] * 4 + [anywhere] * 4,
        out_specs=(anywhere,) * 3 + (vmem,) * 2,
        scratch_shapes=[
            pltpu.VMEM((ROWS, WIDTH), BF16),
            pltpu.VMEM((2, 2 * ROWS, 384), BF16),
            pltpu.VMEM((2, 3 * ROWS, 384), BF16),
            pltpu.VMEM((2, 3 * ROWS, 384), BF16),
            pltpu.VMEM((4, 8, 16, BLOCK), BF16),
            pltpu.VMEM((4, 8, 16, FRONT), BF16),
            pltpu.VMEM((4, 8, 16, BLOCK - FRONT), BF16),
            pltpu.VMEM((4, 8, 16, BLOCK), BF16),
            pltpu.VMEM((3, 4, 4, 4, 96, 384), BF16),
            pltpu.VMEM((3, ROWS, WIDTH), BF16),
            pltpu.VMEM((2, ROWS, 128), BF16),
            pltpu.VMEM((ROWS, 128), BF16),
            pltpu.VMEM((8, ROWS), I32),
            pltpu.VMEM((4, 8, ROWS), I32),
            dma((2, 4)), dma((2, 4)), dma((2, 8)), dma((2, 8)), dma((len(PARTS), 3, 3)), dma((len(PARTS), 3, 3)), dma((3,)), dma((3,)),
            dma((4,)), dma((4,)), dma((4,)), dma((2,)), dma((2,)), dma((2,)), dma((3, 3)), dma((3, 3)), dma((3, 3)), dma((4,)),
        ],
        compiler_params=pltpu.CompilerParams(collective_id=0, has_side_effects=True, vmem_limit_bytes=60 * 2**20),
        name="project_tokens",
    )(target, segment, bucket, mod_table, latents_in, w_query, w_key, w_value)


def attend_kernel(info, q, k, v, seg, out):
    tile = pl.program_id(1)
    begin = (info[tile, 0] // 128) * 128
    span = info[tile, 1] - begin
    base = pl.multiple_of(info[tile, 2], 128)
    seg_query = jnp.transpose(seg[:, pl.ds(base, Q_TILE)].astype(F32))[:, 0:1]

    def over(width):
        start = pl.multiple_of(jnp.minimum(begin, 3 * ROWS - width), 128)
        rows = pl.ds(start, width)
        bias = jnp.where(seg_query == seg[0:1, rows].astype(F32), 0.0, -1e30)
        ones = jnp.ones((width, HEAD_DIM), BF16)
        heads = [(g, slice(e * HEAD_DIM, (e + 1) * HEAD_DIM)) for g in range(2) for e in range(3)]

        def score(g, cols):
            return dot_nt(q[g, 0, :, cols], k[g, 0, rows, cols]) + bias

        ready = score(*heads[0])
        for i, (g, cols) in enumerate(heads):
            scores = ready
            if i + 1 < len(heads):
                ready = score(*heads[i + 1])
            weight = jnp.exp2((scores - jnp.max(scores, axis=1, keepdims=True)) * (HEAD_DIM**-0.5 * LOG2E))
            mixed = dot(weight.astype(BF16), jnp.concatenate([v[g, 0, rows, cols], ones], axis=1))
            out[:, g * 384 + cols.start : g * 384 + cols.stop] = (mixed[:, :HEAD_DIM] / mixed[:, HEAD_DIM:]).astype(BF16)

    least = -1
    for width in SPANS:
        pl.when((span > least) & (span <= width))(functools.partial(over, width))
        least = width


def attend(info, q, k, v, seg):
    return pl.pallas_call(
        attend_kernel,
        out_shape=jax.ShapeDtypeStruct((ROWS, 1536), BF16),
        grid_spec=pltpu.PrefetchScalarGridSpec(
            num_scalar_prefetch=1,
            grid=(2, ROWS // Q_TILE),
            in_specs=[
                pl.BlockSpec((2, 1, Q_TILE, 384), lambda h, t, info: (0, h, t, 0)),
                pl.BlockSpec((2, 1, 3 * ROWS, 384), lambda h, t, info: (0, h, 0, 0)),
                pl.BlockSpec((2, 1, 3 * ROWS, 384), lambda h, t, info: (0, h, 0, 0)),
                pl.BlockSpec((8, 3 * ROWS), lambda h, t, info: (0, 0)),
            ],
            out_specs=pl.BlockSpec((Q_TILE, 768), lambda h, t, info: (t, h)),
        ),
        compiler_params=pltpu.CompilerParams(vmem_limit_bytes=60 * 2**20),
        name="attend",
    )(info, q, k, v, seg)


def on_device(latents, target, segment_ids, clip_bucket, mod_table, w_query, w_key, w_value):
    q, k, v, seg, info = project_tokens(
        target.reshape(1, ROWS), segment_ids, clip_bucket, mod_table, latents, w_query, w_key, w_value
    )
    return attend(info, q, k, v, seg)


def solution(mesh):
    in_specs = (
        P(("dp", "seq"), None),
        P(("dp", "seq")),
        P("dp", "seq"),
        P("dp", None),
        P(),
        P("dp", "seq"),
        P("dp", "seq"),
        P("dp", "seq"),
    )
    out_specs = P(("dp", "seq"), None)
    return jax.shard_map(on_device, mesh=mesh, in_specs=in_specs, out_specs=out_specs, check_vma=False)
```
